512 devices in a mesh: layer: 64 (over z, y), tok: 8 (over x, core).
Axes of the slice: x: 4, y: 8, z: 8, core: 2. Of those that a mesh axis runs over, the one named last changes fastest.
Arguments:
- states: bfloat16 [64, 1024, 1024], P('layer', 'tok'), may hold values from -6 to 6
- w_qkv: bfloat16 [128, 1024, 1536], P('layer', 'tok'), may hold values from -12 to 12
- w_out: bfloat16 [128, 512, 1024], P('layer', 'tok'), may hold values from -0.25 to 0.25
- gains: float32 [128, 1024], P('layer'), may hold values from 0.5 to 1.5
- coarse_gain: float32 [64, 1024], P('layer'), may hold values from 0.85 to 1
- doc_ids: int32 [1024], P('tok'), may hold values from 0 to 3, never falling along the last dimension, each value on 1 to 512 neighbouring positions
Outputs:
- corrected: float32 [64, 1024, 1024], P('layer', 'tok')
- ends: float32 [64, 1024, 1024], P('layer', 'tok')
The draws below stay inside these ranges and needn't reach their ends.
Inputs may be any that keep to these rules, and one draw needn't show every extreme that they name: `doc_ids`: document numbers never fall along the tokens; each document has 1 to 512 tokens and one has exactly 512.
All inputs are finite; a program needn't handle non-finite values.
Results may differ from the reference program's by a relative error of at most 0.0065.
Values may be sent and summed in bfloat16 or wider, within the bound.
A program may use at most 128 MiB of HBM per device.

```python
import math
import jax
import jax.numpy as jnp
import numpy as np
from jax import lax

D = 1024
HEADS = 8
HEAD_DIM = 64
HD = 512
SLABS = 64
LAYERS = 128
TOKENS = 1024


def draw_states(key, part):
    base = jax.random.normal(jax.random.fold_in(key, 11), (SLABS, TOKENS, D), jnp.float32)
    return jnp.clip(base, -6.0, 6.0).astype(jnp.bfloat16)


def draw_w_qkv(key, part):
    base = jax.random.normal(jax.random.fold_in(key, 21), (LAYERS, D, 3 * HD), jnp.float32)
    base = jnp.clip(base, -6.0, 6.0) * float(D) ** (-0.5)
    return base.astype(jnp.bfloat16)


def level_of(stream_key, extent, pieces, low, high):
    level, own = 1.0, jax.random.fold_in(stream_key, 6)
    for dim, shards_of in pieces:
        steps = jnp.exp(jax.random.uniform(jax.random.fold_in(own, dim), (shards_of,), jnp.float32, low / len(pieces), high / len(pieces)))
        level = level * jnp.repeat(steps, extent[dim] // shards_of).reshape([-1 if axis == dim else 1 for axis in range(len(extent))])
    return level


def length_profile(number_of, total, reach, lean):
    portions = [(1 << 20) // math.isqrt(rank ** lean) + 1 for rank in range(2, number_of + 1)]
    surplus, counts = total - reach - (number_of - 1), [1] * (number_of - 1)
    while surplus > 0:
        movable = [i for i in range(number_of - 1) if counts[i] < reach]
        whole, budget = sum([portions[i] for i in movable]), surplus
        for i in movable:
            addition = min(reach - counts[i], max(1, budget * portions[i] // whole), surplus)
            counts[i] = counts[i] + addition
            surplus = surplus - addition
    return np.array([reach] + counts)


def uneven_parts(own_key, count, total, limit, skew):
    if count == 2:
        one = jax.random.randint(own_key, (), max(1, total - limit), min(limit, total - 1) + 1)
        return jnp.stack([one, total - one])
    tallies = jnp.asarray(length_profile(count, total, limit, skew), jnp.int32)
    couples = (count - 1) // 2
    donor, receiver = tallies[1:1 + 2 * couples:2], tallies[2:2 + 2 * couples:2]
    slack = jnp.minimum(donor - 1, limit - receiver)
    shifted = jax.random.randint(jax.random.fold_in(own_key, 1), (couples,), 0, 1 << 20) % (slack + 1)
    tallies = tallies.at[1:1 + 2 * couples:2].set(donor - shifted).at[2:2 + 2 * couples:2].set(receiver + shifted)
    return tallies[jax.random.permutation(jax.random.fold_in(own_key, 2), count)]


def normal_values(stream_key, extent, deviation, most, split=(), held_as=jnp.bfloat16):
    level = level_of(stream_key, extent, split, -0.22, 0.18) if split else 1.0
    array = jax.random.normal(stream_key, extent, jnp.float32) * deviation * level
    return jnp.minimum(jnp.maximum(array, -most), most).astype(held_as)


def setup_inputs(seed: int = 0) -> dict:
    seeds = jax.random.split(jax.random.key(seed), 7)
    states = draw_states(jax.random.fold_in(seeds[6], 71), 0)
    w_qkv = draw_w_qkv(jax.random.fold_in(seeds[6], 71), 0)
    w_out = normal_values(seeds[2], (LAYERS, HD, D), HD ** -0.5, 0.25, ((0, 64), (1, 8)))
    gains = jnp.clip(1.0 + 0.1 * jax.random.normal(seeds[3], (LAYERS, D), jnp.float32), 0.5, 1.5)
    coarse_gain = jnp.clip(jnp.exp(math.log(1.0) - 0.1625189 * jax.random.uniform(seeds[4], (SLABS, D), jnp.float32) ** level_of(seeds[4], (SLABS, D), ((0, 64),), -0.2, 0.2)), 0.85, 1.0)
    doc_ids = jnp.searchsorted(jnp.cumsum(uneven_parts(seeds[5], 4, TOKENS, TOKENS // 2, 0)), jnp.arange(TOKENS), side="right").astype(jnp.int32)
    return dict(states=states, w_qkv=w_qkv, w_out=w_out, gains=gains, coarse_gain=coarse_gain, doc_ids=doc_ids)


def apply_layer(state, weight_qkv, weight_out, gain, doc_ids):
    count = state.shape[0]
    width = HD
    mean_square = lax.optimization_barrier(jnp.mean(state * state, axis=1, keepdims=True))
    normed = (state * lax.rsqrt(mean_square + 1e-05) * gain[None, :]).astype(jnp.bfloat16)
    qkv = jnp.dot(normed, weight_qkv, preferred_element_type=jnp.float32).astype(jnp.bfloat16)
    query = qkv[:, :width].reshape(count, HEADS, HEAD_DIM).astype(jnp.float32)
    keys = qkv[:, width:2 * width].reshape(count, HEADS, HEAD_DIM).astype(jnp.float32)
    values = qkv[:, 2 * width:].reshape(count, HEADS, HEAD_DIM).astype(jnp.float32)
    scores = jnp.einsum('qhd,khd->hqk', query, keys) / jnp.sqrt(jnp.float32(HEAD_DIM))
    position = jnp.arange(count, dtype=jnp.int32)
    allowed = (position[None, :] <= position[:, None]) & (doc_ids[None, :] == doc_ids[:, None])
    scores = jnp.where(allowed[None], scores, -1e+30)
    peak = lax.optimization_barrier(jnp.max(scores, axis=2, keepdims=True))
    expo = jnp.where(allowed[None], jnp.exp(scores - peak), 0.0)
    probs = (expo / lax.optimization_barrier(jnp.sum(expo, axis=2, keepdims=True))).astype(jnp.bfloat16)
    mixed = jnp.einsum('hqk,khd->qhd', probs.astype(jnp.float32), values)
    mixed = mixed.reshape(count, width).astype(jnp.bfloat16)
    return state + jnp.dot(mixed, weight_out, preferred_element_type=jnp.float32)

def reference(states, w_qkv, w_out, gains, coarse_gain, doc_ids):
    slabs = states.shape[0]
    depth = w_qkv.shape[0] // slabs

    def relax(index):
        state = states[index].astype(jnp.float32)
        for inner in range(depth):
            layer_id = index * depth + inner
            state = apply_layer(state, w_qkv[layer_id], w_out[layer_id], gains[layer_id], doc_ids)
        return state
    leaving = lax.map(relax, jnp.arange(slabs, dtype=jnp.int32))
    follow = jnp.concatenate([states[1:].astype(jnp.float32), jnp.zeros((1,) + states.shape[1:], jnp.float32)], axis=0)
    residual = leaving - follow

    def sweep(error, inputs):
        gain_row, resid = inputs
        return (gain_row[None, :] * error + resid, error)
    start = jnp.zeros(states.shape[1:], jnp.float32)
    last, errors = lax.scan(sweep, start, (coarse_gain, residual))
    corrected = states.astype(jnp.float32) + errors
    ends = leaving + coarse_gain[:, None, :] * errors
    return (corrected, ends)
```

```python
import math

import jax
import jax.numpy as jnp
from jax import lax
from jax.experimental import pallas as pl
from jax.experimental.pallas import tpu as pltpu
from jax.sharding import PartitionSpec as P

MESH = pl.DeviceIdType.MESH
D = 1024
NX = 4
NB = 8
RING = 8
CHUNKS = 2
EXP2_SCALE = math.log2(math.e) / 8.0
FAR_FIRST = (4, 3, 5, 2, 6, 1, 7)


def rms(value, gain):
    mean_square = jnp.mean(value * value, axis=1, keepdims=True)
    return (value * lax.rsqrt(mean_square + 1e-05) * gain).astype(jnp.bfloat16)


def make_kernel(ny, nz):
    cw = D // CHUNKS

    def kernel(
        states, w_qkv, w_out, gains, coarse, doc_ids,
        c_out, d_out,
        sx, wq, wo, kv, q2, o1, o2s, o2, x2, nx2, bias, docs,
        gy, pz, dsend, drecv, trecv, csend, crecv,
        loc, w_ss, w_rs, wr_ss, wr_rs, s_ss, s_rs, doc_ss, doc_rs,
        wo_ss, wo_rs, wor_ss, wor_rs, kv_ss, kv_rs, o1_ss, o1_rs, o2_ss, o2_rs,
        g_ss, g_rs, p_ss, p_rs, y1_ss, y1_rs, z_ss, z_rs, y2_ss, y2_rs,
    ):
        layer, tok = lax.axis_index("layer"), lax.axis_index("tok")
        x, c = tok // 2, tok % 2
        z, y = layer // ny, layer % ny
        sibling = (layer, 2 * x + 1 - c)

        def chip(delta):
            return (x + delta) % NX

        def at_x(delta):
            return (layer, 2 * chip(delta) + c)

        def at_y(delta):
            return (z * ny + (y + delta) % ny, tok)

        def at_z(delta):
            return (((z + delta) % nz) * ny + y, tok)

        ydeltas = [k for k in FAR_FIRST if k < ny]
        zdeltas = [k for k in FAR_FIRST if k < nz]
        sends = []

        def remote(src, dst, ss, rs, device):
            copy = pltpu.make_async_remote_copy(
                src_ref=src, dst_ref=dst, send_sem=ss, recv_sem=rs,
                device_id=device, device_id_type=MESH,
            )
            return copy

        def send(*args):
            copy = remote(*args)
            copy.start()
            sends.append(copy)
            return copy

        own_state = pltpu.make_async_copy(states.at[0], sx.at[x], loc.at[0])
        own_state.start()
        own_wq = [[], []]
        own_wo = []
        for inner in range(2):
            for part in range(3):
                copy = pltpu.make_async_copy(
                    w_qkv.at[inner, :, pl.ds(pl.multiple_of(part * 512 + 128 * x, 128), 128)],
                    wq.at[inner, x, c, :, pl.ds(128 * part, 128)],
                    loc.at[1 + 3 * inner + part],
                )
                copy.start()
                own_wq[inner].append(copy)
            copy = pltpu.make_async_copy(w_out.at[inner], wo.at[inner, x, c], loc.at[7 + inner])
            copy.start()
            own_wo.append(copy)
        docs[tok] = doc_ids[...]
        gy[y] = coarse[...]

        barrier = pltpu.get_barrier_semaphore()
        partners = [sibling] + [at_x(k) for k in (2, 1, 3)]
        partners += [at_y(k) for k in ydeltas] + [at_z(k) for k in zdeltas]
        for partner in partners:
            pl.semaphore_signal(barrier, inc=1, device_id=partner, device_id_type=MESH)
        pl.semaphore_wait(barrier, len(partners))

        def send_wq(inner):
            found = []
            for delta in (2, 1, 3):
                for part in range(3):
                    found.append(send(
                        w_qkv.at[inner, :, pl.ds(pl.multiple_of(part * 512 + 128 * chip(delta), 128), 128)],
                        wq.at[inner, x, c, :, pl.ds(128 * part, 128)],
                        w_ss.at[inner, delta, part], w_rs.at[inner, delta, part], at_x(delta),
                    ))
            return found

        def share_wq(inner, arriving):
            for copy in own_wq[inner]:
                copy.wait()
            for copy in arriving:
                copy.wait_recv()
            return send(wq.at[inner, :, c], wq.at[inner, :, c], wr_ss.at[inner], wr_rs.at[inner], sibling)

        def send_wo(inner):
            return [
                send(w_out.at[inner], wo.at[inner, x, c], wo_ss.at[inner, k], wo_rs.at[inner, k], at_x(k))
                for k in (2, 1, 3)
            ]

        def share_wo(inner, arriving):
            own_wo[inner].wait()
            for copy in arriving:
                copy.wait_recv()
            return send(wo.at[inner, :, c], wo.at[inner, :, c], wor_ss.at[inner], wor_rs.at[inner], sibling)

        wq_coming = send_wq(0)
        doc_coming = [
            send(doc_ids, docs.at[tok], doc_ss.at[k], doc_rs.at[k], at_x(k)) for k in (2, 1, 3)
        ]

        def half(delta, number):
            rows = pl.ds(64 * number, 64)
            return send(
                states.at[0, rows], sx.at[x, rows], s_ss.at[delta, number], s_rs.at[delta, number], at_x(delta)
            )

        from_left_0, from_right_1 = half(1, 0), half(3, 1)
        from_left_1, from_right_0 = half(1, 1), half(3, 0)
        gain_coming = [send(coarse, gy.at[y], g_ss.at[k], g_rs.at[k], at_y(k)) for k in ydeltas]

        for copy in doc_coming:
            copy.wait_recv()
        doc_shared = [
            send(docs.at[2 * k + c], docs.at[2 * k + c], doc_ss.at[4 + k], doc_rs.at[4 + k], sibling)
            for k in range(NX)
        ]
        for copy in gain_coming:
            copy.wait_recv()
        product = gy[0]
        for k in range(1, ny):
            product = product * gy[k]
        pz[z] = product
        product_coming = [send(pz.at[z], pz.at[z], p_ss.at[k], p_rs.at[k], at_z(k)) for k in zdeltas]
        for copy in doc_shared:
            copy.wait_recv()

        key_first = [0, 0, c, 2 + c]
        key_blocks = [2, 4, 5, 5]
        row = lax.broadcasted_iota(jnp.int32, (128, 128), 0)
        lane = lax.broadcasted_iota(jnp.int32, (128, 128), 1)
        for j in range(NX):
            block = 2 * j + c
            mine = docs[block].astype(jnp.float32)
            mine = jnp.broadcast_to(mine, (128, 128)).T
            for k in range(key_blocks[j]):
                other = key_first[j] + k
                theirs = docs[other].astype(jnp.float32)
                allowed = (mine == theirs) & (lane + 128 * (other - block) <= row)
                bias[j, :, 128 * k : 128 * (k + 1)] = jnp.where(allowed, 0.0, -1e30)

        wq_shared = share_wq(0, wq_coming)

        from_left_0.wait_recv()
        left_two = send(
            sx.at[chip(3), pl.ds(0, 64)], sx.at[chip(3), pl.ds(0, 64)], s_ss.at[2, 0], s_rs.at[2, 0], at_x(1)
        )
        from_right_1.wait_recv()
        right_two = send(
            sx.at[chip(1), pl.ds(64, 64)], sx.at[chip(1), pl.ds(64, 64)], s_ss.at[2, 1], s_rs.at[2, 1], at_x(3)
        )
        wo_coming = send_wo(0)
        wq_shared.wait_recv()
        own_state.wait()

        kv_shared = [[], []]

        def keep_qkv(inner, j, qkv):
            head = lax.broadcasted_iota(jnp.int32, (128, 128), 1) < 64
            query = qkv[:, :128]
            q2[j, :128] = jnp.where(head, query, 0.0).astype(jnp.bfloat16)
            q2[j, 128:] = jnp.where(head, 0.0, query).astype(jnp.bfloat16)
            block = 2 * j + c
            kv[inner, block] = qkv[:, 128:].astype(jnp.bfloat16)

        def first_qkv(delta):
            j = chip(delta)
            normed = rms(sx[j].astype(jnp.float32), gains[0:1, :])
            qkv = jnp.dot(normed, wq[0].reshape(D, 384), preferred_element_type=jnp.float32)
            keep_qkv(0, j, qkv)
            block = 2 * j + c
            kv_shared[0].append(
                send(kv.at[0, block], kv.at[0, block], kv_ss.at[0, delta], kv_rs.at[0, delta], sibling)
            )

        first_qkv(0)
        from_left_1.wait_recv()
        first_qkv(3)
        from_right_0.wait_recv()
        first_qkv(1)
        left_two.wait_recv()
        right_two.wait_recv()
        first_qkv(2)

        def attention(inner, j):
            count = 128 * key_blocks[j]
            keys = pl.ds(key_first[j], key_blocks[j])
            k = kv[inner, keys, :, :128].reshape(count, 128)
            v = kv[inner, keys, :, 128:].reshape(count, 128)
            scores = lax.dot_general(
                q2[j], k, (((1,), (1,)), ((), ())), preferred_element_type=jnp.float32
            )
            scores = (scores.reshape(2, 128, count) + bias[j, :, :count][None]).reshape(256, count)
            peak = jnp.max(scores, axis=1, keepdims=True)
            expo = jnp.exp2((scores - peak) * EXP2_SCALE)
            total = jnp.sum(expo, axis=1, keepdims=True)
            probs = (expo * (1.0 / total)).astype(jnp.bfloat16)
            mixed = jnp.dot(probs, v, preferred_element_type=jnp.float32)
            head = lax.broadcasted_iota(jnp.int32, (128, 128), 1) < 64
            return jnp.where(head, mixed[:128], mixed[128:]).astype(jnp.bfloat16)

        for copy in kv_shared[0]:
            copy.wait_recv()
        o1_coming = []
        for j in range(NX):
            o1[x, j] = attention(0, j)
            o1_coming.append([
                send(o1.at[x, j], o1.at[x, j], o1_ss.at[j, k], o1_rs.at[j, k], at_x(k)) for k in (2, 1, 3)
            ])
        wq_coming = send_wq(1)
        wo_shared = share_wo(0, wo_coming)
        wo_coming = send_wo(1)
        wo_shared.wait_recv()

        for j in range(NX):
            for copy in o1_coming[j]:
                copy.wait_recv()
            heads = jnp.concatenate([o1[k, j] for k in range(NX)], axis=1)
            value = sx[j].astype(jnp.float32) + jnp.dot(
                heads, wo[0].reshape(512, D), preferred_element_type=jnp.float32
            )
            x2[j] = value
            nx2[j] = rms(value, gains[1:2, :])

        share_wq(1, wq_coming).wait_recv()
        for j in range(NX):
            qkv = jnp.dot(nx2[j], wq[1].reshape(D, 384), preferred_element_type=jnp.float32)
            keep_qkv(1, j, qkv)
            block = 2 * j + c
            kv_shared[1].append(
                send(kv.at[1, block], kv.at[1, block], kv_ss.at[1, j], kv_rs.at[1, j], sibling)
            )
        for copy in kv_shared[1]:
            copy.wait_recv()
        home = []
        for j in range(NX):
            o2s[j] = attention(1, j)
            copy = remote(o2s.at[j], o2.at[x], o2_ss.at[j], o2_rs.at[x], (layer, 2 * j + c))
            home.append(copy)

            @pl.when(x != j)
            def _(copy=copy):
                copy.start()

        o2[x] = o2s[x]
        share_wo(1, wo_coming).wait_recv()
        for delta in (1, 2, 3):
            pltpu.make_async_copy(o2s.at[0], o2.at[chip(delta)], o2_rs.at[chip(delta)]).wait()
        heads = jnp.concatenate([o2[k] for k in range(NX)], axis=1)
        value = x2[x] + jnp.dot(heads, wo[1].reshape(512, D), preferred_element_type=jnp.float32)
        start = jnp.where(layer == 0, 0.0, sx[x].astype(jnp.float32))
        value = value - coarse[...] * start
        d_out[...] = value
        dsend[...] = value.astype(jnp.bfloat16)

        def columns(chunk):
            return pl.ds(cw * chunk, cw)

        def rows_of(position):
            return pl.ds(pl.multiple_of(16 * position, 16), 16)

        y1_coming = [
            [
                send(
                    dsend.at[rows_of((y + k) % ny), columns(chunk)], drecv.at[y, :, columns(chunk)],
                    y1_ss.at[chunk, k], y1_rs.at[chunk, k], at_y(k),
                )
                for k in ydeltas
            ]
            for chunk in range(CHUNKS)
        ]
        drecv[y] = dsend[rows_of(y), :]
        for copy in product_coming:
            copy.wait_recv()
        z_coming = []
        for chunk in range(CHUNKS):
            for copy in y1_coming[chunk]:
                copy.wait_recv()
            total = jnp.zeros((16, cw), jnp.float32)
            for k in range(ny):
                total = gy[k, :, columns(chunk)] * total + drecv[k, :, columns(chunk)].astype(jnp.float32)
            trecv[z, :, columns(chunk)] = total.astype(jnp.bfloat16)
            z_coming.append([
                send(
                    trecv.at[z, :, columns(chunk)], trecv.at[z, :, columns(chunk)],
                    z_ss.at[chunk, k], z_rs.at[chunk, k], at_z(k),
                )
                for k in zdeltas
            ])
        y2_coming = []
        for chunk in range(CHUNKS):
            for copy in z_coming[chunk]:
                copy.wait_recv()
            carry = jnp.zeros((16, cw), jnp.float32)
            for k in range(nz):
                longer = pz[k, :, columns(chunk)] * carry + trecv[k, :, columns(chunk)].astype(jnp.float32)
                carry = jnp.where(k < z, longer, carry)
            for k in range(ny):
                csend[k, :, columns(chunk)] = carry.astype(jnp.bfloat16)
                carry = gy[k, :, columns(chunk)] * carry + drecv[k, :, columns(chunk)].astype(jnp.float32)
            crecv[rows_of(y), columns(chunk)] = csend[y, :, columns(chunk)]
            y2_coming.append([
                send(
                    csend.at[(y + k) % ny, :, columns(chunk)], crecv.at[rows_of(y), columns(chunk)],
                    y2_ss.at[chunk, k], y2_rs.at[chunk, k], at_y(k),
                )
                for k in ydeltas
            ])
        for chunk in range(CHUNKS):
            for copy in y2_coming[chunk]:
                copy.wait_recv()
        c_out[...] = crecv[...]
        for copy in sends:
            copy.wait_send()
        for j in range(NX):

            @pl.when(x != j)
            def _(copy=home[j]):
                copy.wait_send()

    bf16, f32 = jnp.bfloat16, jnp.float32
    dma = pltpu.SemaphoreType.DMA
    scratch = [
        pltpu.VMEM((NX, 128, D), bf16),
        pltpu.VMEM((2, NX, 2, 128, 384), bf16),
        pltpu.VMEM((2, NX, 2, 64, D), bf16),
        pltpu.VMEM((2, NB, 128, 256), bf16),
        pltpu.VMEM((NX, 256, 128), bf16),
        pltpu.VMEM((NX, NX, 128, 128), bf16),
        pltpu.VMEM((NX, 128, 128), bf16),
        pltpu.VMEM((NX, 128, 128), bf16),
        pltpu.VMEM((NX, 128, D), f32),
        pltpu.VMEM((NX, 128, D), bf16),
        pltpu.VMEM((NX, 128, 640), f32),
        pltpu.VMEM((NB, 1, 128), jnp.int32),
        pltpu.VMEM((ny, 1, D), f32),
        pltpu.VMEM((nz, 1, D), f32),
        pltpu.VMEM((128, D), bf16),
        pltpu.VMEM((ny, 16, D), bf16),
        pltpu.VMEM((nz, 16, D), bf16),
        pltpu.VMEM((ny, 16, D), bf16),
        pltpu.VMEM((128, D), bf16),
        dma((9,)),
        dma((2, 4, 3)), dma((2, 4, 3)), dma((2,)), dma((2,)),
        dma((4, 2)), dma((4, 2)), dma((8,)), dma((8,)),
        dma((2, 4)), dma((2, 4)), dma((2,)), dma((2,)),
        dma((2, 4)), dma((2, 4)), dma((4, 4)), dma((4, 4)), dma((4,)), dma((4,)),
        dma((8,)), dma((8,)), dma((8,)), dma((8,)),
        dma((CHUNKS, 8)), dma((CHUNKS, 8)), dma((CHUNKS, 8)), dma((CHUNKS, 8)), dma((CHUNKS, 8)), dma((CHUNKS, 8)),
    ]
    anywhere, vmem = pl.BlockSpec(memory_space=pl.ANY), pl.BlockSpec(memory_space=pltpu.VMEM)
    return pl.pallas_call(
        kernel,
        out_shape=(jax.ShapeDtypeStruct((128, D), bf16), jax.ShapeDtypeStruct((128, D), f32)),
        in_specs=[anywhere] * 3 + [vmem] * 3,
        out_specs=(vmem, vmem),
        scratch_shapes=scratch,
        compiler_params=pltpu.CompilerParams(
            collective_id=0, has_side_effects=True, vmem_limit_bytes=40 << 20
        ),
        cost_estimate=pl.CostEstimate(
            flops=3_000_000_000, bytes_accessed=4_000_000, transcendentals=2_000_000
        ),
    )


def solution(mesh):
    layers = mesh.shape["layer"]
    ny = min(RING, layers)
    nz = layers // ny
    call = make_kernel(ny, nz)

    def per_device(states, w_qkv, w_out, gains, coarse_gain, doc_ids):
        entering, source = call(states, w_qkv, w_out, gains, coarse_gain, doc_ids.reshape(1, -1))
        first = lax.axis_index("layer") == 0
        entering = entering.astype(jnp.float32)
        state = states[0].astype(jnp.float32)
        corrected = entering + jnp.where(first, state, 0.0)
        ends = coarse_gain * entering + source
        return corrected[None], ends[None]

    in_specs = (
        P("layer", "tok", None),
        P("layer", "tok", None),
        P("layer", "tok", None),
        P("layer", None),
        P("layer", None),
        P("tok"),
    )
    out_specs = (P("layer", "tok", None), P("layer", "tok", None))
    return jax.shard_map(
        per_device, mesh=mesh, in_specs=in_specs, out_specs=out_specs, check_vma=False
    )
```

```python
import math

import jax
import jax.numpy as jnp
from jax import lax
from jax.experimental import pallas as pl
from jax.experimental.pallas import tpu as pltpu
from jax.sharding import PartitionSpec as P

MESH = pl.DeviceIdType.MESH
D = 1024
NX = 4
NB = 8
RING = 8
CHUNKS = 4
EXP2_SCALE = math.log2(math.e) / 8.0
FAR_FIRST = (4, 3, 5, 2, 6, 1, 7)


def rms(value, gain):
    mean_square = jnp.mean(value * value, axis=1, keepdims=True)
    return (value * lax.rsqrt(mean_square + 1e-05) * gain).astype(jnp.bfloat16)


def make_kernel(ny, nz):
    cw = D // CHUNKS

    def kernel(
        states, w_qkv, w_out, gains_in, coarse_in, doc_ids,
        c_out, d_out,
        sx, wq, wo, kv, q2, o1, o2s, o2, x2, bias, docs,
        gains, gy, pz, dsend, drecv, trecv, csend, crecv,
        loc, w_ss, w_rs, wr_ss, wr_rs, s_ss, s_rs, doc_ss, doc_rs,
        wo_ss, wo_rs, wor_ss, wor_rs, kv_ss, kv_rs, o1_ss, o1_rs, o2_ss, o2_rs,
        g_ss, g_rs, p_ss, p_rs, y1_ss, y1_rs, z_ss, z_rs, y2_ss, y2_rs,
    ):
        layer, tok = lax.axis_index("layer"), lax.axis_index("tok")
        x, c = tok // 2, tok % 2
        z, y = layer // ny, layer % ny
        sibling = (layer, 2 * x + 1 - c)

        def chip(delta):
            return (x + delta) % NX

        def at_x(delta):
            return (layer, 2 * chip(delta) + c)

        def at_y(delta):
            return (z * ny + (y + delta) % ny, tok)

        def at_z(delta):
            return (((z + delta) % nz) * ny + y, tok)

        ydeltas = [k for k in FAR_FIRST if k < ny]
        zdeltas = [k for k in FAR_FIRST if k < nz]
        sends = []

        def remote(src, dst, ss, rs, device):
            copy = pltpu.make_async_remote_copy(
                src_ref=src, dst_ref=dst, send_sem=ss, recv_sem=rs,
                device_id=device, device_id_type=MESH,
            )
            return copy

        def send(*args):
            copy = remote(*args)
            copy.start()
            sends.append(copy)
            return copy

        own_state = pltpu.make_async_copy(states.at[0], sx.at[x], loc.at[0])
        own_state.start()
        own_wq = [[], []]
        own_wo = []
        for inner in range(2):
            for part in range(3):
                copy = pltpu.make_async_copy(
                    w_qkv.at[inner, :, pl.ds(pl.multiple_of(part * 512 + 128 * x, 128), 128)],
                    wq.at[inner, x, c, :, pl.ds(128 * part, 128)],
                    loc.at[1 + 3 * inner + part],
                )
                copy.start()
                own_wq[inner].append(copy)
            copy = pltpu.make_async_copy(w_out.at[inner], wo.at[inner, x, c], loc.at[7 + inner])
            copy.start()
            own_wo.append(copy)
        own_small = [
            pltpu.make_async_copy(doc_ids, docs.at[tok], loc.at[9]),
            pltpu.make_async_copy(coarse_in, gy.at[y], loc.at[10]),
            pltpu.make_async_copy(gains_in, gains, loc.at[11]),
        ]
        for copy in own_small:
            copy.start()

        barrier = pltpu.get_barrier_semaphore()
        partners = [sibling] + [at_x(k) for k in (2, 1, 3)]
        partners += [at_y(k) for k in ydeltas] + [at_z(k) for k in zdeltas]
        for partner in partners:
            pl.semaphore_signal(barrier, inc=1, device_id=partner, device_id_type=MESH)
        for copy in own_small:
            copy.wait()
        pl.semaphore_wait(barrier, len(partners))

        def send_wq_to(inner, delta):
            return [
                send(
                    w_qkv.at[inner, :, pl.ds(pl.multiple_of(part * 512 + 128 * chip(delta), 128), 128)],
                    wq.at[inner, x, c, :, pl.ds(128 * part, 128)],
                    w_ss.at[inner, delta, part], w_rs.at[inner, delta, part], at_x(delta),
                )
                for part in range(3)
            ]

        def share_wq(inner, arriving):
            for copy in own_wq[inner]:
                copy.wait()
            for copy in arriving:
                copy.wait_recv()
            return send(wq.at[inner, :, c], wq.at[inner, :, c], wr_ss.at[inner], wr_rs.at[inner], sibling)

        def send_wo(inner):
            def part(delta, number):
                rows = pl.ds(32 * number, 32)
                return send(
                    w_out.at[inner, rows], wo.at[inner, x, c, rows],
                    wo_ss.at[inner, delta, number], wo_rs.at[inner, delta, number], at_x(delta),
                )

            return part(1, 0), part(3, 1), part(1, 1), part(3, 0)

        def forward_wo(inner, arriving):
            found = [arriving[2], arriving[3]]
            for number, origin, target in ((0, 3, 1), (1, 1, 3)):
                arriving[number].wait_recv()
                block = wo.at[inner, chip(origin), c, pl.ds(32 * number, 32)]
                found.append(send(block, block, wo_ss.at[inner, 2, number], wo_rs.at[inner, 2, number], at_x(target)))
            return found

        def share_wo(inner, arriving):
            own_wo[inner].wait()
            for copy in arriving:
                copy.wait_recv()
            return send(wo.at[inner, :, c], wo.at[inner, :, c], wor_ss.at[inner], wor_rs.at[inner], sibling)

        wq_coming = send_wq_to(0, 2) + send_wq_to(0, 1) + send_wq_to(0, 3)
        doc_coming = [
            send(docs.at[tok], docs.at[tok], doc_ss.at[k], doc_rs.at[k], at_x(k)) for k in (2, 1, 3)
        ]

        def half(delta, number):
            rows = pl.ds(64 * number, 64)
            return send(
                states.at[0, rows], sx.at[x, rows], s_ss.at[delta, number], s_rs.at[delta, number], at_x(delta)
            )

        from_left_0, from_right_1 = half(1, 0), half(3, 1)
        from_left_1, from_right_0 = half(1, 1), half(3, 0)
        gain_coming = [send(gy.at[y], gy.at[y], g_ss.at[k], g_rs.at[k], at_y(k)) for k in ydeltas]

        for copy in doc_coming:
            copy.wait_recv()
        doc_shared = [
            send(docs.at[2 * k + c], docs.at[2 * k + c], doc_ss.at[4 + k], doc_rs.at[4 + k], sibling)
            for k in range(NX)
        ]
        for copy in gain_coming:
            copy.wait_recv()
        product = gy[0]
        for k in range(1, ny):
            product = product * gy[k]
        pz[z] = product
        product_coming = [send(pz.at[z], pz.at[z], p_ss.at[k], p_rs.at[k], at_z(k)) for k in zdeltas]
        for copy in doc_shared:
            copy.wait_recv()

        key_first = [0, 0, c, 2 + c]
        key_blocks = [2, 4, 5, 5]
        row = lax.broadcasted_iota(jnp.int32, (128, 128), 0)
        lane = lax.broadcasted_iota(jnp.int32, (128, 128), 1)
        for j in range(NX):
            block = 2 * j + c
            mine = docs[block].astype(jnp.float32)
            mine = jnp.broadcast_to(mine, (128, 128)).T
            for k in range(key_blocks[j]):
                other = key_first[j] + k
                theirs = docs[other].astype(jnp.float32)
                allowed = (mine == theirs) & (lane + 128 * (other - block) <= row)
                bias[j, :, 128 * k : 128 * (k + 1)] = jnp.where(allowed, 0.0, -1e30)

        wq_shared = share_wq(0, wq_coming)

        from_left_0.wait_recv()
        left_two = send(
            sx.at[chip(3), pl.ds(0, 64)], sx.at[chip(3), pl.ds(0, 64)], s_ss.at[2, 0], s_rs.at[2, 0], at_x(1)
        )
        from_right_1.wait_recv()
        right_two = send(
            sx.at[chip(1), pl.ds(64, 64)], sx.at[chip(1), pl.ds(64, 64)], s_ss.at[2, 1], s_rs.at[2, 1], at_x(3)
        )
        wo_coming = send_wo(0)
        wq_shared.wait_recv()
        own_state.wait()

        kv_shared = [[], []]

        def keep_qkv(inner, j, qkv):
            head = lax.broadcasted_iota(jnp.int32, (128, 128), 1) < 64
            query = qkv[:, :128]
            q2[j, :128] = jnp.where(head, query, 0.0).astype(jnp.bfloat16)
            q2[j, 128:] = jnp.where(head, 0.0, query).astype(jnp.bfloat16)
            block = 2 * j + c
            kv[inner, block] = qkv[:, 128:].astype(jnp.bfloat16)

        def first_qkv(delta):
            j = chip(delta)
            normed = rms(sx[j].astype(jnp.float32), gains[0:1, :])
            qkv = jnp.dot(normed, wq[0].reshape(D, 384), preferred_element_type=jnp.float32)
            keep_qkv(0, j, qkv)
            block = 2 * j + c
            kv_shared[0].append(
                send(kv.at[0, block], kv.at[0, block], kv_ss.at[0, delta], kv_rs.at[0, delta], sibling)
            )

        first_qkv(0)
        from_left_1.wait_recv()
        first_qkv(3)
        from_right_0.wait_recv()
        first_qkv(1)
        left_two.wait_recv()
        right_two.wait_recv()
        first_qkv(2)
        wo_coming = forward_wo(0, wo_coming)
        wq_coming = send_wq_to(1, 2) + send_wq_to(1, 1) + send_wq_to(1, 3)

        def attention(inner, j):
            count = 128 * key_blocks[j]
            keys = pl.ds(key_first[j], key_blocks[j])
            k = kv[inner, keys, :, :128].reshape(count, 128)
            v = kv[inner, keys, :, 128:].reshape(count, 128)
            scores = lax.dot_general(
                q2[j], k, (((1,), (1,)), ((), ())), preferred_element_type=jnp.float32
            )
            scores = (scores.reshape(2, 128, count) + bias[j, :, :count][None]).reshape(256, count)
            peak = jnp.max(scores, axis=1, keepdims=True)
            expo = jnp.exp2((scores - peak) * EXP2_SCALE)
            total = jnp.sum(expo, axis=1, keepdims=True)
            probs = (expo * (1.0 / total)).astype(jnp.bfloat16)
            mixed = jnp.dot(probs, v, preferred_element_type=jnp.float32)
            head = lax.broadcasted_iota(jnp.int32, (128, 128), 1) < 64
            return jnp.where(head, mixed[:128], mixed[128:]).astype(jnp.bfloat16)

        for copy in kv_shared[0]:
            copy.wait_recv()
        o1_coming = []
        for j in range(NX):
            o1[x, j] = attention(0, j)
            o1_coming.append([
                send(o1.at[x, j], o1.at[x, j], o1_ss.at[j, k], o1_rs.at[j, k], at_x(k)) for k in (1, 3)
            ])

        def forward_o1(j):
            came, origin, target = (0, 3, 1) if j < 2 else (1, 1, 3)
            o1_coming[j][came].wait_recv()
            block = o1.at[chip(origin), j]
            passed = send(block, block, o1_ss.at[j, 2], o1_rs.at[j, 2], at_x(target))
            o1_coming[j] = [o1_coming[j][1 - came], passed]

        wo_shared = share_wo(0, wo_coming)
        for j in range(NX):
            forward_o1(j)
        wo_coming = send_wo(1)
        wq_shared = share_wq(1, wq_coming)
        wo_shared.wait_recv()

        for j in range(NX):
            for copy in o1_coming[j]:
                copy.wait_recv()
            heads = jnp.concatenate([o1[k, j] for k in range(NX)], axis=1)
            value = sx[j].astype(jnp.float32) + jnp.dot(
                heads, wo[0].reshape(512, D), preferred_element_type=jnp.float32
            )
            x2[j] = value
            if j == 0:
                wq_shared.wait_recv()
            qkv = jnp.dot(rms(value, gains[1:2, :]), wq[1].reshape(D, 384), preferred_element_type=jnp.float32)
            keep_qkv(1, j, qkv)
            block = 2 * j + c
            kv_shared[1].append(
                send(kv.at[1, block], kv.at[1, block], kv_ss.at[1, j], kv_rs.at[1, j], sibling)
            )
        for copy in kv_shared[1]:
            copy.wait_recv()
        wo_coming = forward_wo(1, wo_coming)
        home = []
        for j in range(NX):
            o2s[j] = attention(1, j)
            copy = remote(o2s.at[j], o2.at[x], o2_ss.at[j], o2_rs.at[x], (layer, 2 * j + c))
            home.append(copy)

            @pl.when(x != j)
            def _(copy=copy):
                copy.start()

        o2[x] = o2s[x]
        share_wo(1, wo_coming).wait_recv()
        for delta in (1, 2, 3):
            pltpu.make_async_copy(o2s.at[0], o2.at[chip(delta)], o2_rs.at[chip(delta)]).wait()
        heads = jnp.concatenate([o2[k] for k in range(NX)], axis=1)
        value = x2[x] + jnp.dot(heads, wo[1].reshape(512, D), preferred_element_type=jnp.float32)
        start = jnp.where(layer == 0, 0.0, sx[x].astype(jnp.float32))
        value = value - gy[y] * start
        d_out[...] = value
        dsend[...] = value.astype(jnp.bfloat16)

        def columns(chunk):
            return pl.ds(cw * chunk, cw)

        def rows_of(position):
            return pl.ds(pl.multiple_of(16 * position, 16), 16)

        y1_coming = [
            [
                send(
                    dsend.at[rows_of((y + k) % ny), columns(chunk)], drecv.at[y, :, columns(chunk)],
                    y1_ss.at[chunk, k], y1_rs.at[chunk, k], at_y(k),
                )
                for k in ydeltas
            ]
            for chunk in range(CHUNKS)
        ]
        drecv[y] = dsend[rows_of(y), :]
        for copy in product_coming:
            copy.wait_recv()
        z_coming = []
        for chunk in range(CHUNKS):
            for copy in y1_coming[chunk]:
                copy.wait_recv()
            total = jnp.zeros((16, cw), jnp.float32)
            for k in range(ny):
                total = gy[k, :, columns(chunk)] * total + drecv[k, :, columns(chunk)].astype(jnp.float32)
            trecv[z, :, columns(chunk)] = total.astype(jnp.bfloat16)
            z_coming.append([
                send(
                    trecv.at[z, :, columns(chunk)], trecv.at[z, :, columns(chunk)],
                    z_ss.at[chunk, k], z_rs.at[chunk, k], at_z(k),
                )
                for k in zdeltas
            ])
        y2_coming = []
        for chunk in range(CHUNKS):
            for copy in z_coming[chunk]:
                copy.wait_recv()
            carry = jnp.zeros((16, cw), jnp.float32)
            for k in range(nz):
                longer = pz[k, :, columns(chunk)] * carry + trecv[k, :, columns(chunk)].astype(jnp.float32)
                carry = jnp.where(k < z, longer, carry)
            for k in range(ny):
                csend[k, :, columns(chunk)] = carry.astype(jnp.bfloat16)
                carry = gy[k, :, columns(chunk)] * carry + drecv[k, :, columns(chunk)].astype(jnp.float32)
            crecv[rows_of(y), columns(chunk)] = csend[y, :, columns(chunk)]
            y2_coming.append([
                send(
                    csend.at[(y + k) % ny, :, columns(chunk)], crecv.at[rows_of(y), columns(chunk)],
                    y2_ss.at[chunk, k], y2_rs.at[chunk, k], at_y(k),
                )
                for k in ydeltas
            ])
        for chunk in range(CHUNKS):
            for copy in y2_coming[chunk]:
                copy.wait_recv()
        c_out[...] = crecv[...]
        for copy in sends:
            copy.wait_send()
        for j in range(NX):

            @pl.when(x != j)
            def _(copy=home[j]):
                copy.wait_send()

    bf16, f32 = jnp.bfloat16, jnp.float32
    dma = pltpu.SemaphoreType.DMA
    scratch = [
        pltpu.VMEM((NX, 128, D), bf16),
        pltpu.VMEM((2, NX, 2, 128, 384), bf16),
        pltpu.VMEM((2, NX, 2, 64, D), bf16),
        pltpu.VMEM((2, NB, 128, 256), bf16),
        pltpu.VMEM((NX, 256, 128), bf16),
        pltpu.VMEM((NX, NX, 128, 128), bf16),
        pltpu.VMEM((NX, 128, 128), bf16),
        pltpu.VMEM((NX, 128, 128), bf16),
        pltpu.VMEM((NX, 128, D), f32),
        pltpu.VMEM((NX, 128, 640), f32),
        pltpu.VMEM((NB, 1, 128), jnp.int32),
        pltpu.VMEM((2, D), f32),
        pltpu.VMEM((ny, 1, D), f32),
        pltpu.VMEM((nz, 1, D), f32),
        pltpu.VMEM((128, D), bf16),
        pltpu.VMEM((ny, 16, D), bf16),
        pltpu.VMEM((nz, 16, D), bf16),
        pltpu.VMEM((ny, 16, D), bf16),
        pltpu.VMEM((128, D), bf16),
        dma((12,)),
        dma((2, 4, 3)), dma((2, 4, 3)), dma((2,)), dma((2,)),
        dma((4, 2)), dma((4, 2)), dma((8,)), dma((8,)),
        dma((2, 4, 2)), dma((2, 4, 2)), dma((2,)), dma((2,)),
        dma((2, 4)), dma((2, 4)), dma((4, 4)), dma((4, 4)), dma((4,)), dma((4,)),
        dma((8,)), dma((8,)), dma((8,)), dma((8,)),
        dma((CHUNKS, 8)), dma((CHUNKS, 8)), dma((CHUNKS, 8)), dma((CHUNKS, 8)), dma((CHUNKS, 8)), dma((CHUNKS, 8)),
    ]
    anywhere, vmem = pl.BlockSpec(memory_space=pltpu.HBM), pl.BlockSpec(memory_space=pltpu.VMEM)
    return pl.pallas_call(
        kernel,
        out_shape=(jax.ShapeDtypeStruct((128, D), bf16), jax.ShapeDtypeStruct((128, D), f32)),
        in_specs=[anywhere] * 6,
        out_specs=(vmem, vmem),
        scratch_shapes=scratch,
        compiler_params=pltpu.CompilerParams(
            collective_id=0, has_side_effects=True, vmem_limit_bytes=60 << 20
        ),
        cost_estimate=pl.CostEstimate(
            flops=3_000_000_000, bytes_accessed=4_000_000, transcendentals=2_000_000
        ),
    )


def solution(mesh):
    layers = mesh.shape["layer"]
    ny = min(RING, layers)
    nz = layers // ny
    call = make_kernel(ny, nz)

    def per_device(states, w_qkv, w_out, gains, coarse_gain, doc_ids):
        entering, source = call(states, w_qkv, w_out, gains, coarse_gain, doc_ids.reshape(1, -1))
        first = lax.axis_index("layer") == 0
        entering = entering.astype(jnp.float32)
        state = states[0].astype(jnp.float32)
        corrected = entering + jnp.where(first, state, 0.0)
        ends = coarse_gain * entering + source
        return corrected[None], ends[None]

    in_specs = (
        P("layer", "tok", None),
        P("layer", "tok", None),
        P("layer", "tok", None),
        P("layer", None),
        P("layer", None),
        P("tok"),
    )
    out_specs = (P("layer", "tok", None), P("layer", "tok", None))
    return jax.shard_map(
        per_device, mesh=mesh, in_specs=in_specs, out_specs=out_specs, check_vma=False
    )
```

```python
import math

import jax
import jax.numpy as jnp
from jax import lax
from jax.experimental import pallas as pl
from jax.experimental.pallas import tpu as pltpu
from jax.sharding import PartitionSpec as P

MESH = pl.DeviceIdType.MESH
D = 1024
NX = 4
NB = 8
RING = 8
CHUNKS = 4
EXP2_SCALE = math.log2(math.e) / 8.0
FAR_FIRST = (4, 3, 5, 2, 6, 1, 7)


def rms(value, gain):
    mean_square = jnp.mean(value * value, axis=1, keepdims=True)
    return (value * lax.rsqrt(mean_square + 1e-05) * gain).astype(jnp.bfloat16)


def make_kernel(ny, nz):
    cw = D // CHUNKS

    def kernel(
        states, w_qkv, w_out, gains_in, coarse_in, doc_ids,
        c_out, d_out,
        sx, wq, wo, kv, q2, o1, o2s, o2, x2, bias, docs,
        gains, gy, pz, dsend, drecv, trecv, csend, crecv,
        loc, w_ss, w_rs, wr_ss, wr_rs, s_ss, s_rs, doc_ss, doc_rs,
        wo_ss, wo_rs, wor_ss, wor_rs, kv_ss, kv_rs, o1_ss, o1_rs, o2_ss, o2_rs,
        g_ss, g_rs, p_ss, p_rs, y1_ss, y1_rs, z_ss, z_rs, y2_ss, y2_rs,
    ):
        layer, tok = lax.axis_index("layer"), lax.axis_index("tok")
        x, c = tok // 2, tok % 2
        z, y = layer // ny, layer % ny
        sibling = (layer, 2 * x + 1 - c)

        def chip(delta):
            return (x + delta) % NX

        def at_x(delta):
            return (layer, 2 * chip(delta) + c)

        def at_y(delta):
            return (z * ny + (y + delta) % ny, tok)

        def at_z(delta):
            return (((z + delta) % nz) * ny + y, tok)

        ydeltas = [k for k in FAR_FIRST if k < ny]
        zdeltas = [k for k in FAR_FIRST if k < nz]
        sends = []

        def remote(src, dst, ss, rs, device):
            copy = pltpu.make_async_remote_copy(
                src_ref=src, dst_ref=dst, send_sem=ss, recv_sem=rs,
                device_id=device, device_id_type=MESH,
            )
            return copy

        def send(*args):
            copy = remote(*args)
            copy.start()
            sends.append(copy)
            return copy

        own_state = pltpu.make_async_copy(states.at[0], sx.at[x], loc.at[0])
        own_state.start()
        own_wq = [[], []]
        own_wo = []
        for inner in range(2):
            for part in range(3):
                copy = pltpu.make_async_copy(
                    w_qkv.at[inner, :, pl.ds(pl.multiple_of(part * 512 + 128 * x, 128), 128)],
                    wq.at[inner, x, c, :, pl.ds(128 * part, 128)],
                    loc.at[1 + 3 * inner + part],
                )
                copy.start()
                own_wq[inner].append(copy)
            copy = pltpu.make_async_copy(w_out.at[inner], wo.at[inner, x, c], loc.at[7 + inner])
            copy.start()
            own_wo.append(copy)
        own_small = [
            pltpu.make_async_copy(doc_ids, docs.at[tok], loc.at[9]),
            pltpu.make_async_copy(coarse_in, gy.at[y], loc.at[10]),
            pltpu.make_async_copy(gains_in, gains, loc.at[11]),
        ]
        for copy in own_small:
            copy.start()

        barrier = pltpu.get_barrier_semaphore()
        partners = [sibling] + [at_x(k) for k in (2, 1, 3)]
        partners += [at_y(k) for k in ydeltas] + [at_z(k) for k in zdeltas]
        for partner in partners:
            pl.semaphore_signal(barrier, inc=1, device_id=partner, device_id_type=MESH)
        for copy in own_small:
            copy.wait()
        pl.semaphore_wait(barrier, len(partners))

        def send_wq_to(inner, delta):
            return [
                send(
                    w_qkv.at[inner, :, pl.ds(pl.multiple_of(part * 512 + 128 * chip(delta), 128), 128)],
                    wq.at[inner, x, c, :, pl.ds(128 * part, 128)],
                    w_ss.at[inner, delta, part], w_rs.at[inner, delta, part], at_x(delta),
                )
                for part in range(3)
            ]

        def share_wq(inner, arriving):
            for copy in own_wq[inner]:
                copy.wait()
            for copy in arriving:
                copy.wait_recv()
            return send(wq.at[inner, :, c], wq.at[inner, :, c], wr_ss.at[inner], wr_rs.at[inner], sibling)

        def send_wo(inner):
            def part(delta, number):
                rows = pl.ds(32 * number, 32)
                return send(
                    w_out.at[inner, rows], wo.at[inner, x, c, rows],
                    wo_ss.at[inner, delta, number], wo_rs.at[inner, delta, number], at_x(delta),
                )

            return part(1, 0), part(3, 1), part(1, 1), part(3, 0)

        def forward_wo(inner, arriving):
            found = [arriving[2], arriving[3]]
            for number, origin, target in ((0, 3, 1), (1, 1, 3)):
                arriving[number].wait_recv()
                block = wo.at[inner, chip(origin), c, pl.ds(32 * number, 32)]
                found.append(send(block, block, wo_ss.at[inner, 2, number], wo_rs.at[inner, 2, number], at_x(target)))
            return found

        def share_wo(inner, arriving):
            own_wo[inner].wait()
            for copy in arriving:
                copy.wait_recv()
            return send(wo.at[inner, :, c], wo.at[inner, :, c], wor_ss.at[inner], wor_rs.at[inner], sibling)

        wq_coming = send_wq_to(0, 2) + send_wq_to(0, 1) + send_wq_to(0, 3)
        doc_coming = [
            send(docs.at[tok], docs.at[tok], doc_ss.at[k], doc_rs.at[k], at_x(k)) for k in (2, 1, 3)
        ]

        def half(delta, number):
            rows = pl.ds(64 * number, 64)
            return send(
                states.at[0, rows], sx.at[x, rows], s_ss.at[delta, number], s_rs.at[delta, number], at_x(delta)
            )

        from_left_0, from_right_1 = half(1, 0), half(3, 1)
        from_left_1, from_right_0 = half(1, 1), half(3, 0)
        gain_coming = [send(gy.at[y], gy.at[y], g_ss.at[k], g_rs.at[k], at_y(k)) for k in ydeltas]

        for copy in doc_coming:
            copy.wait_recv()
        doc_shared = [
            send(docs.at[2 * k + c], docs.at[2 * k + c], doc_ss.at[4 + k], doc_rs.at[4 + k], sibling)
            for k in range(NX)
        ]
        for copy in gain_coming:
            copy.wait_recv()
        product = gy[0]
        for k in range(1, ny):
            product = product * gy[k]
        pz[z] = product
        product_coming = [send(pz.at[z], pz.at[z], p_ss.at[k], p_rs.at[k], at_z(k)) for k in zdeltas]
        for copy in doc_shared:
            copy.wait_recv()

        key_first = [0, 0, c, 2 + c]
        key_blocks = [2, 4, 5, 5]
        row = lax.broadcasted_iota(jnp.int32, (128, 128), 0)
        lane = lax.broadcasted_iota(jnp.int32, (128, 128), 1)
        for j in range(NX):
            block = 2 * j + c
            mine = docs[block].astype(jnp.float32)
            mine = jnp.broadcast_to(mine, (128, 128)).T
            for k in range(key_blocks[j]):
                other = key_first[j] + k
                theirs = docs[other].astype(jnp.float32)
                allowed = (mine == theirs) & (lane + 128 * (other - block) <= row)
                bias[j, :, 128 * k : 128 * (k + 1)] = jnp.where(allowed, 0.0, -1e30)

        wq_shared = share_wq(0, wq_coming)

        from_left_0.wait_recv()
        left_two = send(
            sx.at[chip(3), pl.ds(0, 64)], sx.at[chip(3), pl.ds(0, 64)], s_ss.at[2, 0], s_rs.at[2, 0], at_x(1)
        )
        from_right_1.wait_recv()
        right_two = send(
            sx.at[chip(1), pl.ds(64, 64)], sx.at[chip(1), pl.ds(64, 64)], s_ss.at[2, 1], s_rs.at[2, 1], at_x(3)
        )
        wo_coming = send_wo(0)
        wq_shared.wait_recv()
        own_state.wait()

        kv_shared = [[], []]

        def keep_qkv(inner, j, qkv):
            head = lax.broadcasted_iota(jnp.int32, (128, 128), 1) < 64
            query = qkv[:, :128]
            q2[j, :128] = jnp.where(head, query, 0.0).astype(jnp.bfloat16)
            q2[j, 128:] = jnp.where(head, 0.0, query).astype(jnp.bfloat16)
            block = 2 * j + c
            kv[inner, block] = qkv[:, 128:].astype(jnp.bfloat16)

        def first_qkv(delta):
            j = chip(delta)
            normed = rms(sx[j].astype(jnp.float32), gains[0:1, :])
            qkv = jnp.dot(normed, wq[0].reshape(D, 384), preferred_element_type=jnp.float32)
            keep_qkv(0, j, qkv)
            block = 2 * j + c
            kv_shared[0].append(
                send(kv.at[0, block], kv.at[0, block], kv_ss.at[0, delta], kv_rs.at[0, delta], sibling)
            )

        first_qkv(0)
        from_left_1.wait_recv()
        first_qkv(3)
        from_right_0.wait_recv()
        first_qkv(1)
        left_two.wait_recv()
        right_two.wait_recv()
        first_qkv(2)
        wo_coming = forward_wo(0, wo_coming)
        wq_coming = send_wq_to(1, 2) + send_wq_to(1, 1) + send_wq_to(1, 3)

        def attention(inner, j):
            count = 128 * key_blocks[j]
            keys = pl.ds(key_first[j], key_blocks[j])
            k = kv[inner, keys, :, :128].reshape(count, 128)
            v = kv[inner, keys, :, 128:].reshape(count, 128)
            scores = lax.dot_general(
                q2[j], k, (((1,), (1,)), ((), ())), preferred_element_type=jnp.float32
            )
            scores = (scores.reshape(2, 128, count) + bias[j, :, :count][None]).reshape(256, count)
            peak = jnp.max(scores, axis=1, keepdims=True)
            expo = jnp.exp2((scores - peak) * EXP2_SCALE)
            total = jnp.sum(expo, axis=1, keepdims=True)
            probs = (expo * (1.0 / total)).astype(jnp.bfloat16)
            mixed = jnp.dot(probs, v, preferred_element_type=jnp.float32)
            head = lax.broadcasted_iota(jnp.int32, (128, 128), 1) < 64
            return jnp.where(head, mixed[:128], mixed[128:]).astype(jnp.bfloat16)

        for copy in kv_shared[0]:
            copy.wait_recv()
        o1_coming = []
        for j in range(NX):
            o1[x, j] = attention(0, j)
            o1_coming.append([
                send(o1.at[x, j], o1.at[x, j], o1_ss.at[j, k], o1_rs.at[j, k], at_x(k)) for k in (2, 1, 3)
            ])

        wo_next = send_wo(1)
        wo_shared = share_wo(0, wo_coming)
        wo_coming = wo_next
        wq_shared = share_wq(1, wq_coming)
        wo_shared.wait_recv()

        for j in range(NX):
            for copy in o1_coming[j]:
                copy.wait_recv()
            heads = jnp.concatenate([o1[k, j] for k in range(NX)], axis=1)
            value = sx[j].astype(jnp.float32) + jnp.dot(
                heads, wo[0].reshape(512, D), preferred_element_type=jnp.float32
            )
            x2[j] = value
            if j == 3:
                wo_coming = forward_wo(1, wo_coming)
            if j == 0:
                wq_shared.wait_recv()
            qkv = jnp.dot(rms(value, gains[1:2, :]), wq[1].reshape(D, 384), preferred_element_type=jnp.float32)
            keep_qkv(1, j, qkv)
            block = 2 * j + c
            kv_shared[1].append(
                send(kv.at[1, block], kv.at[1, block], kv_ss.at[1, j], kv_rs.at[1, j], sibling)
            )
        for copy in kv_shared[1]:
            copy.wait_recv()
        home = []
        for j in range(NX):
            if j == 3:
                wo_shared = share_wo(1, wo_coming)
            o2s[j] = attention(1, j)
            copy = remote(o2s.at[j], o2.at[x], o2_ss.at[j], o2_rs.at[x], (layer, 2 * j + c))
            home.append(copy)

            @pl.when(x != j)
            def _(copy=copy):
                copy.start()

        o2[x] = o2s[x]
        wo_shared.wait_recv()
        for delta in (1, 2, 3):
            pltpu.make_async_copy(o2s.at[0], o2.at[chip(delta)], o2_rs.at[chip(delta)]).wait()
        heads = jnp.concatenate([o2[k] for k in range(NX)], axis=1)
        value = x2[x] + jnp.dot(heads, wo[1].reshape(512, D), preferred_element_type=jnp.float32)
        start = jnp.where(layer == 0, 0.0, sx[x].astype(jnp.float32))
        value = value - gy[y] * start
        d_out[...] = value
        dsend[...] = value.astype(jnp.bfloat16)

        def columns(chunk):
            return pl.ds(cw * chunk, cw)

        def rows_of(position):
            return pl.ds(pl.multiple_of(16 * position, 16), 16)

        y1_coming = [
            [
                send(
                    dsend.at[rows_of((y + k) % ny), columns(chunk)], drecv.at[y, :, columns(chunk)],
                    y1_ss.at[chunk, k], y1_rs.at[chunk, k], at_y(k),
                )
                for k in ydeltas
            ]
            for chunk in range(CHUNKS)
        ]
        drecv[y] = dsend[rows_of(y), :]
        for copy in product_coming:
            copy.wait_recv()
        z_coming = []
        for chunk in range(CHUNKS):
            for copy in y1_coming[chunk]:
                copy.wait_recv()
            total = jnp.zeros((16, cw), jnp.float32)
            for k in range(ny):
                total = gy[k, :, columns(chunk)] * total + drecv[k, :, columns(chunk)].astype(jnp.float32)
            trecv[z, :, columns(chunk)] = total.astype(jnp.bfloat16)
            z_coming.append([
                send(
                    trecv.at[z, :, columns(chunk)], trecv.at[z, :, columns(chunk)],
                    z_ss.at[chunk, k], z_rs.at[chunk, k], at_z(k),
                )
                for k in zdeltas
            ])
        y2_coming = []
        for chunk in range(CHUNKS):
            for copy in z_coming[chunk]:
                copy.wait_recv()
            carry = jnp.zeros((16, cw), jnp.float32)
            for k in range(nz):
                longer = pz[k, :, columns(chunk)] * carry + trecv[k, :, columns(chunk)].astype(jnp.float32)
                carry = jnp.where(k < z, longer, carry)
            for k in range(ny):
                csend[k, :, columns(chunk)] = carry.astype(jnp.bfloat16)
                carry = gy[k, :, columns(chunk)] * carry + drecv[k, :, columns(chunk)].astype(jnp.float32)
            crecv[rows_of(y), columns(chunk)] = csend[y, :, columns(chunk)]
            y2_coming.append([
                send(
                    csend.at[(y + k) % ny, :, columns(chunk)], crecv.at[rows_of(y), columns(chunk)],
                    y2_ss.at[chunk, k], y2_rs.at[chunk, k], at_y(k),
                )
                for k in ydeltas
            ])
        for chunk in range(CHUNKS):
            for copy in y2_coming[chunk]:
                copy.wait_recv()
        c_out[...] = crecv[...]
        for copy in sends:
            copy.wait_send()
        for j in range(NX):

            @pl.when(x != j)
            def _(copy=home[j]):
                copy.wait_send()

    bf16, f32 = jnp.bfloat16, jnp.float32
    dma = pltpu.SemaphoreType.DMA
    scratch = [
        pltpu.VMEM((NX, 128, D), bf16),
        pltpu.VMEM((2, NX, 2, 128, 384), bf16),
        pltpu.VMEM((2, NX, 2, 64, D), bf16),
        pltpu.VMEM((2, NB, 128, 256), bf16),
        pltpu.VMEM((NX, 256, 128), bf16),
        pltpu.VMEM((NX, NX, 128, 128), bf16),
        pltpu.VMEM((NX, 128, 128), bf16),
        pltpu.VMEM((NX, 128, 128), bf16),
        pltpu.VMEM((NX, 128, D), f32),
        pltpu.VMEM((NX, 128, 640), f32),
        pltpu.VMEM((NB, 1, 128), jnp.int32),
        pltpu.VMEM((2, D), f32),
        pltpu.VMEM((ny, 1, D), f32),
        pltpu.VMEM((nz, 1, D), f32),
        pltpu.VMEM((128, D), bf16),
        pltpu.VMEM((ny, 16, D), bf16),
        pltpu.VMEM((nz, 16, D), bf16),
        pltpu.VMEM((ny, 16, D), bf16),
        pltpu.VMEM((128, D), bf16),
        dma((12,)),
        dma((2, 4, 3)), dma((2, 4, 3)), dma((2,)), dma((2,)),
        dma((4, 2)), dma((4, 2)), dma((8,)), dma((8,)),
        dma((2, 4, 2)), dma((2, 4, 2)), dma((2,)), dma((2,)),
        dma((2, 4)), dma((2, 4)), dma((4, 4)), dma((4, 4)), dma((4,)), dma((4,)),
        dma((8,)), dma((8,)), dma((8,)), dma((8,)),
        dma((CHUNKS, 8)), dma((CHUNKS, 8)), dma((CHUNKS, 8)), dma((CHUNKS, 8)), dma((CHUNKS, 8)), dma((CHUNKS, 8)),
    ]
    anywhere, vmem = pl.BlockSpec(memory_space=pltpu.HBM), pl.BlockSpec(memory_space=pltpu.VMEM)
    return pl.pallas_call(
        kernel,
        out_shape=(jax.ShapeDtypeStruct((128, D), bf16), jax.ShapeDtypeStruct((128, D), f32)),
        in_specs=[anywhere] * 6,
        out_specs=(vmem, vmem),
        scratch_shapes=scratch,
        compiler_params=pltpu.CompilerParams(
            collective_id=0, has_side_effects=True, vmem_limit_bytes=40 << 20
        ),
        cost_estimate=pl.CostEstimate(
            flops=3_000_000_000, bytes_accessed=4_000_000, transcendentals=2_000_000
        ),
    )


def solution(mesh):
    layers = mesh.shape["layer"]
    ny = min(RING, layers)
    nz = layers // ny
    call = make_kernel(ny, nz)

    def per_device(states, w_qkv, w_out, gains, coarse_gain, doc_ids):
        hold = [pltpu.with_memory_space_constraint(v, pltpu.HBM) for v in (states, w_qkv, w_out, gains, coarse_gain, doc_ids.reshape(1, -1))]
        entering, source = call(*hold)
        first = lax.axis_index("layer") == 0
        entering = entering.astype(jnp.float32)
        state = states[0].astype(jnp.float32)
        corrected = entering + jnp.where(first, state, 0.0)
        ends = coarse_gain * entering + source
        return corrected[None], ends[None]

    in_specs = (
        P("layer", "tok", None),
        P("layer", "tok", None),
        P("layer", "tok", None),
        P("layer", None),
        P("layer", None),
        P("tok"),
    )
    out_specs = (P("layer", "tok", None), P("layer", "tok", None))
    return jax.shard_map(
        per_device, mesh=mesh, in_specs=in_specs, out_specs=out_specs, check_vma=False
    )
```

```python
import math

import jax
import jax.numpy as jnp
from jax import lax
from jax.experimental import pallas as pl
from jax.experimental.pallas import tpu as pltpu
from jax.sharding import PartitionSpec as P

MESH = pl.DeviceIdType.MESH
D = 1024
NX = 4
NB = 8
RING = 8
CHUNKS = 4
EXP2_SCALE = math.log2(math.e) / 8.0
FAR_FIRST = (4, 3, 5, 2, 6, 1, 7)


def rms(value, gain):
    mean_square = jnp.mean(value * value, axis=1, keepdims=True)
    return (value * lax.rsqrt(mean_square + 1e-05) * gain).astype(jnp.bfloat16)


def make_kernel(ny, nz):
    cw = D // CHUNKS

    def kernel(
        states, w_qkv, w_out, gains_in, coarse_in, doc_ids,
        c_out, d_out,
        sx, wq, wo, kv, q2, o1, o2s, o2, x2, bias, docs,
        gains, gy, pz, dsend, drecv, trecv, csend, crecv,
        loc, w_ss, w_rs, wr_ss, wr_rs, s_ss, s_rs, doc_ss, doc_rs,
        wo_ss, wo_rs, wor_ss, wor_rs, kv_ss, kv_rs, o1_ss, o1_rs, o2_ss, o2_rs,
        g_ss, g_rs, p_ss, p_rs, y1_ss, y1_rs, z_ss, z_rs, y2_ss, y2_rs,
    ):
        layer, tok = lax.axis_index("layer"), lax.axis_index("tok")
        x, c = lax.div(tok, 2), lax.rem(tok, 2)
        z, y = lax.div(layer, ny), lax.rem(layer, ny)
        sibling = (layer, 2 * x + 1 - c)

        chips = [lax.rem(x + k, NX) for k in range(NX)]
        ring_y = [lax.rem(y + k, ny) for k in range(ny)]
        ring_z = [lax.rem(z + k, nz) for k in range(nz)]

        def chip(delta):
            return chips[delta]

        def at_x(delta):
            return (layer, 2 * chips[delta] + c)

        def at_y(delta):
            return (z * ny + ring_y[delta], tok)

        def at_z(delta):
            return (ring_z[delta] * ny + y, tok)

        ydeltas = [k for k in FAR_FIRST if k < ny]
        zdeltas = [k for k in FAR_FIRST if k < nz]
        sends = []

        def remote(src, dst, ss, rs, device):
            copy = pltpu.make_async_remote_copy(
                src_ref=src, dst_ref=dst, send_sem=ss, recv_sem=rs,
                device_id=device, device_id_type=MESH,
            )
            return copy

        def send(*args):
            copy = remote(*args)
            copy.start()
            sends.append(copy)
            return copy

        own_state = pltpu.make_async_copy(states.at[0], sx.at[x], loc.at[0])
        own_state.start()
        own_wq = [[], []]
        own_wo = []
        for inner in range(2):
            for part in range(3):
                copy = pltpu.make_async_copy(
                    w_qkv.at[inner, :, pl.ds(pl.multiple_of(part * 512 + 128 * x, 128), 128)],
                    wq.at[inner, x, c, :, pl.ds(128 * part, 128)],
                    loc.at[1 + 3 * inner + part],
                )
                copy.start()
                own_wq[inner].append(copy)
            copy = pltpu.make_async_copy(w_out.at[inner], wo.at[inner, x, c], loc.at[7 + inner])
            copy.start()
            own_wo.append(copy)
        own_small = [
            pltpu.make_async_copy(doc_ids, docs.at[tok], loc.at[9]),
            pltpu.make_async_copy(coarse_in, gy.at[y], loc.at[10]),
            pltpu.make_async_copy(gains_in, gains, loc.at[11]),
        ]
        for copy in own_small:
            copy.start()

        barrier = pltpu.get_barrier_semaphore()
        partners = [sibling] + [at_x(k) for k in (2, 1, 3)]
        partners += [at_y(k) for k in ydeltas] + [at_z(k) for k in zdeltas]
        for partner in partners:
            pl.semaphore_signal(barrier, inc=1, device_id=partner, device_id_type=MESH)
        for copy in own_small:
            copy.wait()
        pl.semaphore_wait(barrier, len(partners))

        def send_wq_to(inner, delta):
            return [
                send(
                    w_qkv.at[inner, :, pl.ds(pl.multiple_of(part * 512 + 128 * chip(delta), 128), 128)],
                    wq.at[inner, x, c, :, pl.ds(128 * part, 128)],
                    w_ss.at[inner, delta, part], w_rs.at[inner, delta, part], at_x(delta),
                )
                for part in range(3)
            ]

        def share_wq(inner, arriving):
            for copy in own_wq[inner]:
                copy.wait()
            for copy in arriving:
                copy.wait_recv()
            return send(wq.at[inner, :, c], wq.at[inner, :, c], wr_ss.at[inner], wr_rs.at[inner], sibling)

        def send_wo(inner):
            def part(delta, number):
                rows = pl.ds(32 * number, 32)
                return send(
                    w_out.at[inner, rows], wo.at[inner, x, c, rows],
                    wo_ss.at[inner, delta, number], wo_rs.at[inner, delta, number], at_x(delta),
                )

            return part(1, 0), part(3, 1), part(1, 1), part(3, 0)

        def forward_wo(inner, arriving):
            found = [arriving[2], arriving[3]]
            for number, origin, target in ((0, 3, 1), (1, 1, 3)):
                arriving[number].wait_recv()
                block = wo.at[inner, chip(origin), c, pl.ds(32 * number, 32)]
                found.append(send(block, block, wo_ss.at[inner, 2, number], wo_rs.at[inner, 2, number], at_x(target)))
            return found

        def share_wo(inner, arriving):
            own_wo[inner].wait()
            for copy in arriving:
                copy.wait_recv()
            return send(wo.at[inner, :, c], wo.at[inner, :, c], wor_ss.at[inner], wor_rs.at[inner], sibling)

        wq_coming = send_wq_to(0, 2) + send_wq_to(0, 1) + send_wq_to(0, 3)
        doc_coming = [
            send(docs.at[tok], docs.at[tok], doc_ss.at[k], doc_rs.at[k], at_x(k)) for k in (2, 1, 3)
        ]

        def half(delta, number):
            rows = pl.ds(64 * number, 64)
            return send(
                states.at[0, rows], sx.at[x, rows], s_ss.at[delta, number], s_rs.at[delta, number], at_x(delta)
            )

        from_left_0, from_right_1 = half(1, 0), half(3, 1)
        from_left_1, from_right_0 = half(1, 1), half(3, 0)
        gain_coming = [send(gy.at[y], gy.at[y], g_ss.at[k], g_rs.at[k], at_y(k)) for k in ydeltas]

        for copy in doc_coming:
            copy.wait_recv()
        doc_shared = [
            send(docs.at[2 * k + c], docs.at[2 * k + c], doc_ss.at[4 + k], doc_rs.at[4 + k], sibling)
            for k in range(NX)
        ]
        for copy in gain_coming:
            copy.wait_recv()
        product = gy[0]
        for k in range(1, ny):
            product = product * gy[k]
        pz[z] = product
        product_coming = [send(pz.at[z], pz.at[z], p_ss.at[k], p_rs.at[k], at_z(k)) for k in zdeltas]
        for copy in doc_shared:
            copy.wait_recv()

        key_first = [0, 0, c, 2 + c]
        key_blocks = [2, 4, 5, 5]
        row = lax.broadcasted_iota(jnp.int32, (128, 128), 0)
        lane = lax.broadcasted_iota(jnp.int32, (128, 128), 1)
        for j in range(NX):
            block = 2 * j + c
            mine = docs[block].astype(jnp.float32)
            mine = jnp.broadcast_to(mine, (128, 128)).T
            for k in range(key_blocks[j]):
                other = key_first[j] + k
                theirs = docs[other].astype(jnp.float32)
                allowed = (mine == theirs) & (lane + 128 * (other - block) <= row)
                bias[j, :, 128 * k : 128 * (k + 1)] = jnp.where(allowed, 0.0, -1e30)

        wq_shared = share_wq(0, wq_coming)

        from_left_0.wait_recv()
        left_two = send(
            sx.at[chip(3), pl.ds(0, 64)], sx.at[chip(3), pl.ds(0, 64)], s_ss.at[2, 0], s_rs.at[2, 0], at_x(1)
        )
        from_right_1.wait_recv()
        right_two = send(
            sx.at[chip(1), pl.ds(64, 64)], sx.at[chip(1), pl.ds(64, 64)], s_ss.at[2, 1], s_rs.at[2, 1], at_x(3)
        )
        wo_coming = send_wo(0)
        wq_shared.wait_recv()
        own_state.wait()

        kv_shared = [[], []]

        def keep_qkv(inner, j, qkv):
            head = lax.broadcasted_iota(jnp.int32, (128, 128), 1) < 64
            query = qkv[:, :128]
            q2[j, :128] = jnp.where(head, query, 0.0).astype(jnp.bfloat16)
            q2[j, 128:] = jnp.where(head, 0.0, query).astype(jnp.bfloat16)
            block = 2 * j + c
            kv[inner, block] = qkv[:, 128:].astype(jnp.bfloat16)

        def first_qkv(delta):
            j = chip(delta)
            normed = rms(sx[j].astype(jnp.float32), gains[0:1, :])
            qkv = jnp.dot(normed, wq[0].reshape(D, 384), preferred_element_type=jnp.float32)
            keep_qkv(0, j, qkv)
            block = 2 * j + c
            kv_shared[0].append(
                send(kv.at[0, block], kv.at[0, block], kv_ss.at[0, delta], kv_rs.at[0, delta], sibling)
            )

        first_qkv(0)
        from_left_1.wait_recv()
        first_qkv(3)
        from_right_0.wait_recv()
        first_qkv(1)
        left_two.wait_recv()
        right_two.wait_recv()
        first_qkv(2)
        wo_coming = forward_wo(0, wo_coming)
        wq_coming = send_wq_to(1, 2) + send_wq_to(1, 1) + send_wq_to(1, 3)

        def attention(inner, j):
            count = 128 * key_blocks[j]
            keys = pl.ds(key_first[j], key_blocks[j])
            k = kv[inner, keys, :, :128].reshape(count, 128)
            v = kv[inner, keys, :, 128:].reshape(count, 128)
            scores = lax.dot_general(
                q2[j], k, (((1,), (1,)), ((), ())), preferred_element_type=jnp.float32
            )
            scores = (scores.reshape(2, 128, count) + bias[j, :, :count][None]).reshape(256, count)
            peak = jnp.max(scores, axis=1, keepdims=True)
            expo = jnp.exp2((scores - peak) * EXP2_SCALE)
            total = jnp.sum(expo, axis=1, keepdims=True)
            probs = (expo * (1.0 / total)).astype(jnp.bfloat16)
            mixed = jnp.dot(probs, v, preferred_element_type=jnp.float32)
            head = lax.broadcasted_iota(jnp.int32, (128, 128), 1) < 64
            return jnp.where(head, mixed[:128], mixed[128:]).astype(jnp.bfloat16)

        for copy in kv_shared[0]:
            copy.wait_recv()
        o1_coming = []
        for j in range(NX):
            o1[x, j] = attention(0, j)
            o1_coming.append([
                send(o1.at[x, j], o1.at[x, j], o1_ss.at[j, k], o1_rs.at[j, k], at_x(k)) for k in (2, 1, 3)
            ])

        wo_next = send_wo(1)
        wo_shared = share_wo(0, wo_coming)
        wo_coming = wo_next
        wq_shared = share_wq(1, wq_coming)
        wo_shared.wait_recv()

        for j in range(NX):
            for copy in o1_coming[j]:
                copy.wait_recv()
            heads = jnp.concatenate([o1[k, j] for k in range(NX)], axis=1)
            value = sx[j].astype(jnp.float32) + jnp.dot(
                heads, wo[0].reshape(512, D), preferred_element_type=jnp.float32
            )
            x2[j] = value
            if j == 3:
                wo_coming = forward_wo(1, wo_coming)
            if j == 0:
                wq_shared.wait_recv()
            qkv = jnp.dot(rms(value, gains[1:2, :]), wq[1].reshape(D, 384), preferred_element_type=jnp.float32)
            keep_qkv(1, j, qkv)
            block = 2 * j + c
            kv_shared[1].append(
                send(kv.at[1, block], kv.at[1, block], kv_ss.at[1, j], kv_rs.at[1, j], sibling)
            )
        for copy in kv_shared[1]:
            copy.wait_recv()
        home = []
        for j in range(NX):
            if j == 3:
                wo_shared = share_wo(1, wo_coming)
            o2s[j] = attention(1, j)
            copy = remote(o2s.at[j], o2.at[x], o2_ss.at[j], o2_rs.at[x], (layer, 2 * j + c))
            home.append(copy)

            @pl.when(x != j)
            def _(copy=copy):
                copy.start()

        o2[x] = o2s[x]
        wo_shared.wait_recv()
        for delta in (1, 2, 3):
            pltpu.make_async_copy(o2s.at[0], o2.at[chip(delta)], o2_rs.at[chip(delta)]).wait()
        heads = jnp.concatenate([o2[k] for k in range(NX)], axis=1)
        value = x2[x] + jnp.dot(heads, wo[1].reshape(512, D), preferred_element_type=jnp.float32)
        start = jnp.where(layer == 0, 0.0, sx[x].astype(jnp.float32))
        value = value - gy[y] * start
        d_out[...] = value
        dsend[...] = value.astype(jnp.bfloat16)

        def columns(chunk):
            return pl.ds(cw * chunk, cw)

        def start(*args):
            remote(*args).start()

        def arrived(ref, sem):
            pltpu.make_async_copy(ref, ref, sem).wait()

        def all_of(buffer, count, chunk, sem):
            if count > 1:
                arrived(buffer.at[pl.ds(0, count - 1), :, columns(chunk)], sem.at[chunk])

        def rows_of(position):
            return pl.ds(pl.multiple_of(16 * position, 16), 16)

        for chunk in range(CHUNKS):
            for k in ydeltas:
                start(
                    dsend.at[rows_of(ring_y[k]), columns(chunk)], drecv.at[y, :, columns(chunk)],
                    y1_ss.at[chunk], y1_rs.at[chunk], at_y(k),
                )
        drecv[y] = dsend[rows_of(y), :]
        for copy in product_coming:
            copy.wait_recv()
        for copy in sends:
            copy.wait_send()
        for chunk in range(CHUNKS):
            all_of(drecv, ny, chunk, y1_rs)
            total = jnp.zeros((16, cw), jnp.float32)
            for k in range(ny):
                total = gy[k, :, columns(chunk)] * total + drecv[k, :, columns(chunk)].astype(jnp.float32)
            trecv[z, :, columns(chunk)] = total.astype(jnp.bfloat16)
            for k in zdeltas:
                piece = trecv.at[z, :, columns(chunk)]
                start(piece, piece, z_ss.at[chunk], z_rs.at[chunk], at_z(k))
        for chunk in range(CHUNKS):
            all_of(drecv, ny, chunk, y1_ss)
        for chunk in range(CHUNKS):
            all_of(trecv, nz, chunk, z_rs)
            carry = jnp.zeros((16, cw), jnp.float32)
            for k in range(nz):
                longer = pz[k, :, columns(chunk)] * carry + trecv[k, :, columns(chunk)].astype(jnp.float32)
                carry = jnp.where(k < z, longer, carry)
            for k in range(ny):
                csend[k, :, columns(chunk)] = carry.astype(jnp.bfloat16)
                carry = gy[k, :, columns(chunk)] * carry + drecv[k, :, columns(chunk)].astype(jnp.float32)
            crecv[rows_of(y), columns(chunk)] = csend[y, :, columns(chunk)]
            for k in ydeltas:
                start(
                    csend.at[ring_y[k], :, columns(chunk)], crecv.at[rows_of(y), columns(chunk)],
                    y2_ss.at[chunk], y2_rs.at[chunk], at_y(k),
                )
        for chunk in range(CHUNKS):
            all_of(trecv, nz, chunk, z_ss)
        for j in range(NX):

            @pl.when(x != j)
            def _(copy=home[j]):
                copy.wait_send()

        for chunk in range(CHUNKS):
            all_of(csend, ny, chunk, y2_rs)
        c_out[...] = crecv[...]
        for chunk in range(CHUNKS):
            all_of(csend, ny, chunk, y2_ss)

    bf16, f32 = jnp.bfloat16, jnp.float32
    dma = pltpu.SemaphoreType.DMA
    scratch = [
        pltpu.VMEM((NX, 128, D), bf16),
        pltpu.VMEM((2, NX, 2, 128, 384), bf16),
        pltpu.VMEM((2, NX, 2, 64, D), bf16),
        pltpu.VMEM((2, NB, 128, 256), bf16),
        pltpu.VMEM((NX, 256, 128), bf16),
        pltpu.VMEM((NX, NX, 128, 128), bf16),
        pltpu.VMEM((NX, 128, 128), bf16),
        pltpu.VMEM((NX, 128, 128), bf16),
        pltpu.VMEM((NX, 128, D), f32),
        pltpu.VMEM((NX, 128, 640), f32),
        pltpu.VMEM((NB, 1, 128), jnp.int32),
        pltpu.VMEM((2, D), f32),
        pltpu.VMEM((ny, 1, D), f32),
        pltpu.VMEM((nz, 1, D), f32),
        pltpu.VMEM((128, D), bf16),
        pltpu.VMEM((ny, 16, D), bf16),
        pltpu.VMEM((nz, 16, D), bf16),
        pltpu.VMEM((ny, 16, D), bf16),
        pltpu.VMEM((128, D), bf16),
        dma((12,)),
        dma((2, 4, 3)), dma((2, 4, 3)), dma((2,)), dma((2,)),
        dma((4, 2)), dma((4, 2)), dma((8,)), dma((8,)),
        dma((2, 4, 2)), dma((2, 4, 2)), dma((2,)), dma((2,)),
        dma((2, 4)), dma((2, 4)), dma((4, 4)), dma((4, 4)), dma((4,)), dma((4,)),
        dma((8,)), dma((8,)), dma((8,)), dma((8,)),
        dma((CHUNKS,)), dma((CHUNKS,)), dma((CHUNKS,)), dma((CHUNKS,)), dma((CHUNKS,)), dma((CHUNKS,)),
    ]
    anywhere, vmem = pl.BlockSpec(memory_space=pltpu.HBM), pl.BlockSpec(memory_space=pltpu.VMEM)
    return pl.pallas_call(
        kernel,
        out_shape=(jax.ShapeDtypeStruct((128, D), bf16), jax.ShapeDtypeStruct((128, D), f32)),
        in_specs=[anywhere] * 6,
        out_specs=(vmem, vmem),
        scratch_shapes=scratch,
        compiler_params=pltpu.CompilerParams(
            collective_id=0, has_side_effects=True, vmem_limit_bytes=40 << 20
        ),
        cost_estimate=pl.CostEstimate(
            flops=3_000_000_000, bytes_accessed=4_000_000, transcendentals=2_000_000
        ),
    )


def solution(mesh):
    layers = mesh.shape["layer"]
    ny = min(RING, layers)
    nz = layers // ny
    call = make_kernel(ny, nz)

    def per_device(states, w_qkv, w_out, gains, coarse_gain, doc_ids):
        hold = [pltpu.with_memory_space_constraint(v, pltpu.HBM) for v in (states, w_qkv, w_out, gains, coarse_gain, doc_ids.reshape(1, -1))]
        entering, source = call(*hold)
        first = lax.axis_index("layer") == 0
        entering = entering.astype(jnp.float32)
        state = states[0].astype(jnp.float32)
        corrected = entering + jnp.where(first, state, 0.0)
        ends = coarse_gain * entering + source
        return corrected[None], ends[None]

    in_specs = (
        P("layer", "tok", None),
        P("layer", "tok", None),
        P("layer", "tok", None),
        P("layer", None),
        P("layer", None),
        P("tok"),
    )
    out_specs = (P("layer", "tok", None), P("layer", "tok", None))
    return jax.shard_map(
        per_device, mesh=mesh, in_specs=in_specs, out_specs=out_specs, check_vma=False
    )
```

```python
import math

import jax
import jax.numpy as jnp
from jax import lax
from jax.experimental import pallas as pl
from jax.experimental.pallas import tpu as pltpu
from jax.sharding import PartitionSpec as P

MESH = pl.DeviceIdType.MESH
D = 1024
NX = 4
NB = 8
RING = 8
CHUNKS = 4
EXP2_SCALE = math.log2(math.e) / 8.0
FAR_FIRST = (4, 3, 5, 2, 6, 1, 7)


def rms(value, gain):
    mean_square = jnp.mean(value * value, axis=1, keepdims=True)
    return (value * lax.rsqrt(mean_square + 1e-05) * gain).astype(jnp.bfloat16)


def make_kernel(ny, nz):
    cw = D // CHUNKS

    def kernel(
        states, w_qkv, w_out, gains_in, coarse_in, doc_ids,
        c_out, d_out,
        sx, wq, wo, kv, q2, o1, o2s, o2, x2, bias, docs,
        gains, gy, pz, dsend, drecv, trecv, csend, crecv,
        loc, w_ss, w_rs, wr_ss, wr_rs, s_ss, s_rs, doc_ss, doc_rs,
        wo_ss, wo_rs, wor_ss, wor_rs, kv_ss, kv_rs, o1_ss, o1_rs, o2_ss, o2_rs,
        g_ss, g_rs, p_ss, p_rs, y1_ss, y1_rs, z_ss, z_rs, y2_ss, y2_rs,
    ):
        layer, tok = lax.axis_index("layer"), lax.axis_index("tok")
        x, c = lax.div(tok, 2), lax.rem(tok, 2)
        z, y = lax.div(layer, ny), lax.rem(layer, ny)
        sibling = (layer, 2 * x + 1 - c)

        chips = [lax.rem(x + k, NX) for k in range(NX)]
        ring_y = [lax.rem(y + k, ny) for k in range(ny)]
        ring_z = [lax.rem(z + k, nz) for k in range(nz)]

        def chip(delta):
            return chips[delta]

        def at_x(delta):
            return (layer, 2 * chips[delta] + c)

        def at_y(delta):
            return (z * ny + ring_y[delta], tok)

        def at_z(delta):
            return (ring_z[delta] * ny + y, tok)

        ydeltas = [k for k in FAR_FIRST if k < ny]
        zdeltas = [k for k in FAR_FIRST if k < nz]
        sends = []

        def remote(src, dst, ss, rs, device):
            copy = pltpu.make_async_remote_copy(
                src_ref=src, dst_ref=dst, send_sem=ss, recv_sem=rs,
                device_id=device, device_id_type=MESH,
            )
            return copy

        def send(*args):
            copy = remote(*args)
            copy.start()
            sends.append(copy)
            return copy

        own_state = pltpu.make_async_copy(states.at[0], sx.at[x], loc.at[0])
        own_state.start()
        own_wq = [[], []]
        own_wo = []
        for inner in range(2):
            for part in range(3):
                copy = pltpu.make_async_copy(
                    w_qkv.at[inner, :, pl.ds(pl.multiple_of(part * 512 + 128 * x, 128), 128)],
                    wq.at[inner, x, c, :, pl.ds(128 * part, 128)],
                    loc.at[1 + 3 * inner + part],
                )
                copy.start()
                own_wq[inner].append(copy)
            copy = pltpu.make_async_copy(w_out.at[inner], wo.at[inner, x, c], loc.at[7 + inner])
            copy.start()
            own_wo.append(copy)
        own_small = [
            pltpu.make_async_copy(doc_ids, docs.at[tok], loc.at[9]),
            pltpu.make_async_copy(coarse_in, gy.at[y], loc.at[10]),
            pltpu.make_async_copy(gains_in, gains, loc.at[11]),
        ]
        for copy in own_small:
            copy.start()

        barrier = pltpu.get_barrier_semaphore()
        partners = [sibling] + [at_x(k) for k in (2, 1, 3)]
        partners += [at_y(k) for k in ydeltas] + [at_z(k) for k in zdeltas]
        for partner in partners:
            pl.semaphore_signal(barrier, inc=1, device_id=partner, device_id_type=MESH)
        for copy in own_small:
            copy.wait()
        pl.semaphore_wait(barrier, len(partners))

        def send_wq_to(inner, delta):
            return [
                send(
                    w_qkv.at[inner, :, pl.ds(pl.multiple_of(part * 512 + 128 * chip(delta), 128), 128)],
                    wq.at[inner, x, c, :, pl.ds(128 * part, 128)],
                    w_ss.at[inner, delta, part], w_rs.at[inner, delta, part], at_x(delta),
                )
                for part in range(3)
            ]

        def share_wq(inner, arriving):
            for copy in own_wq[inner]:
                copy.wait()
            for copy in arriving:
                copy.wait_recv()
            return send(wq.at[inner, :, c], wq.at[inner, :, c], wr_ss.at[inner], wr_rs.at[inner], sibling)

        def send_wo(inner):
            def part(delta, number):
                rows = pl.ds(32 * number, 32)
                return send(
                    w_out.at[inner, rows], wo.at[inner, x, c, rows],
                    wo_ss.at[inner, delta, number], wo_rs.at[inner, delta, number], at_x(delta),
                )

            return part(1, 0), part(3, 1), part(1, 1), part(3, 0)

        def forward_wo(inner, arriving):
            found = [arriving[2], arriving[3]]
            for number, origin, target in ((0, 3, 1), (1, 1, 3)):
                arriving[number].wait_recv()
                block = wo.at[inner, chip(origin), c, pl.ds(32 * number, 32)]
                found.append(send(block, block, wo_ss.at[inner, 2, number], wo_rs.at[inner, 2, number], at_x(target)))
            return found

        def share_near(inner, arriving):
            own_wo[inner].wait()
            for copy in arriving[:2]:
                copy.wait_recv()
            return [share_block(inner, k) for k in (0, 1, 3)]

        def share_far(inner, arriving):
            for copy in arriving[2:]:
                copy.wait_recv()
            return [share_block(inner, 2)]

        def share_block(inner, delta):
            block = wo.at[inner, chip(delta), c]
            return send(block, block, wor_ss.at[inner, delta], wor_rs.at[inner, delta], sibling)

        wq_coming = send_wq_to(0, 2) + send_wq_to(0, 1) + send_wq_to(0, 3)
        doc_coming = [
            send(docs.at[tok], docs.at[tok], doc_ss.at[k], doc_rs.at[k], at_x(k)) for k in (2, 1, 3)
        ]

        def half(delta, number):
            rows = pl.ds(64 * number, 64)
            return send(
                states.at[0, rows], sx.at[x, rows], s_ss.at[delta, number], s_rs.at[delta, number], at_x(delta)
            )

        from_left_0, from_right_1 = half(1, 0), half(3, 1)
        from_left_1, from_right_0 = half(1, 1), half(3, 0)
        gain_coming = [send(gy.at[y], gy.at[y], g_ss.at[k], g_rs.at[k], at_y(k)) for k in ydeltas]

        for copy in doc_coming:
            copy.wait_recv()
        doc_shared = [
            send(docs.at[2 * k + c], docs.at[2 * k + c], doc_ss.at[4 + k], doc_rs.at[4 + k], sibling)
            for k in range(NX)
        ]
        for copy in gain_coming:
            copy.wait_recv()
        product = gy[0]
        for k in range(1, ny):
            product = product * gy[k]
        pz[z] = product
        product_coming = [send(pz.at[z], pz.at[z], p_ss.at[k], p_rs.at[k], at_z(k)) for k in zdeltas]
        for copy in doc_shared:
            copy.wait_recv()

        key_first = [0, 0, c, 2 + c]
        key_blocks = [2, 4, 5, 5]
        row = lax.broadcasted_iota(jnp.int32, (128, 128), 0)
        lane = lax.broadcasted_iota(jnp.int32, (128, 128), 1)
        for j in range(NX):
            block = 2 * j + c
            mine = docs[block].astype(jnp.float32)
            mine = jnp.broadcast_to(mine, (128, 128)).T
            for k in range(key_blocks[j]):
                other = key_first[j] + k
                theirs = docs[other].astype(jnp.float32)
                allowed = (mine == theirs) & (lane + 128 * (other - block) <= row)
                bias[j, :, 128 * k : 128 * (k + 1)] = jnp.where(allowed, 0.0, -1e30)

        wq_shared = share_wq(0, wq_coming)

        from_left_0.wait_recv()
        left_two = send(
            sx.at[chip(3), pl.ds(0, 64)], sx.at[chip(3), pl.ds(0, 64)], s_ss.at[2, 0], s_rs.at[2, 0], at_x(1)
        )
        from_right_1.wait_recv()
        right_two = send(
            sx.at[chip(1), pl.ds(64, 64)], sx.at[chip(1), pl.ds(64, 64)], s_ss.at[2, 1], s_rs.at[2, 1], at_x(3)
        )
        wo_coming = send_wo(0)
        wq_shared.wait_recv()
        own_state.wait()

        kv_shared = [[], []]

        def keep_qkv(inner, j, qkv):
            head = lax.broadcasted_iota(jnp.int32, (128, 128), 1) < 64
            query = qkv[:, :128]
            q2[j, :128] = jnp.where(head, query, 0.0).astype(jnp.bfloat16)
            q2[j, 128:] = jnp.where(head, 0.0, query).astype(jnp.bfloat16)
            block = 2 * j + c
            kv[inner, block] = qkv[:, 128:].astype(jnp.bfloat16)

        def first_qkv(delta):
            j = chip(delta)
            normed = rms(sx[j].astype(jnp.float32), gains[0:1, :])
            qkv = jnp.dot(normed, wq[0].reshape(D, 384), preferred_element_type=jnp.float32)
            keep_qkv(0, j, qkv)
            block = 2 * j + c
            kv_shared[0].append(
                send(kv.at[0, block], kv.at[0, block], kv_ss.at[0, delta], kv_rs.at[0, delta], sibling)
            )

        first_qkv(0)
        from_left_1.wait_recv()
        first_qkv(3)
        from_right_0.wait_recv()
        first_qkv(1)
        left_two.wait_recv()
        right_two.wait_recv()
        first_qkv(2)
        wo_coming = forward_wo(0, wo_coming)
        wq_coming = send_wq_to(1, 2) + send_wq_to(1, 1) + send_wq_to(1, 3)

        def attention(inner, j):
            count = 128 * key_blocks[j]
            keys = pl.ds(key_first[j], key_blocks[j])
            k = kv[inner, keys, :, :128].reshape(count, 128)
            v = kv[inner, keys, :, 128:].reshape(count, 128)
            scores = lax.dot_general(
                q2[j], k, (((1,), (1,)), ((), ())), preferred_element_type=jnp.float32
            )
            scores = (scores.reshape(2, 128, count) + bias[j, :, :count][None]).reshape(256, count)
            peak = jnp.max(scores, axis=1, keepdims=True)
            expo = jnp.exp2((scores - peak) * EXP2_SCALE)
            total = jnp.sum(expo, axis=1, keepdims=True)
            probs = (expo * (1.0 / total)).astype(jnp.bfloat16)
            mixed = jnp.dot(probs, v, preferred_element_type=jnp.float32)
            head = lax.broadcasted_iota(jnp.int32, (128, 128), 1) < 64
            return jnp.where(head, mixed[:128], mixed[128:]).astype(jnp.bfloat16)

        for copy in kv_shared[0]:
            copy.wait_recv()
        o1_coming = []
        for j in range(NX):
            o1[x, j] = attention(0, j)
            o1_coming.append([
                send(o1.at[x, j], o1.at[x, j], o1_ss.at[j, k], o1_rs.at[j, k], at_x(k)) for k in (2, 1, 3)
            ])

        wo_next = send_wo(1)
        wo_shared = share_near(0, wo_coming) + share_far(0, wo_coming)
        wo_coming = wo_next
        wq_shared = share_wq(1, wq_coming)
        for copy in wo_shared:
            copy.wait_recv()

        for j in range(NX):
            for copy in o1_coming[j]:
                copy.wait_recv()
            heads = jnp.concatenate([o1[k, j] for k in range(NX)], axis=1)
            value = sx[j].astype(jnp.float32) + jnp.dot(
                heads, wo[0].reshape(512, D), preferred_element_type=jnp.float32
            )
            x2[j] = value
            if j == 3:
                wo_coming = forward_wo(1, wo_coming)
            if j == 0:
                wq_shared.wait_recv()
            qkv = jnp.dot(rms(value, gains[1:2, :]), wq[1].reshape(D, 384), preferred_element_type=jnp.float32)
            keep_qkv(1, j, qkv)
            block = 2 * j + c
            kv_shared[1].append(
                send(kv.at[1, block], kv.at[1, block], kv_ss.at[1, j], kv_rs.at[1, j], sibling)
            )
        for copy in kv_shared[1]:
            copy.wait_recv()
        home = []
        for j in range(NX):
            if j == 2:
                wo_shared = share_near(1, wo_coming)
            if j == 3:
                wo_shared += share_far(1, wo_coming)
            o2s[j] = attention(1, j)
            copy = remote(o2s.at[j], o2.at[x], o2_ss.at[j], o2_rs.at[x], (layer, 2 * j + c))
            home.append(copy)

            @pl.when(x != j)
            def _(copy=copy):
                copy.start()

        o2[x] = o2s[x]
        for copy in wo_shared:
            copy.wait_recv()
        for delta in (1, 2, 3):
            pltpu.make_async_copy(o2s.at[0], o2.at[chip(delta)], o2_rs.at[chip(delta)]).wait()
        heads = jnp.concatenate([o2[k] for k in range(NX)], axis=1)

        def columns(chunk):
            return pl.ds(cw * chunk, cw)

        def start(*args):
            remote(*args).start()

        def arrived(ref, sem):
            pltpu.make_async_copy(ref, ref, sem).wait()

        def all_of(buffer, count, chunk, sem):
            if count > 1:
                arrived(buffer.at[pl.ds(0, count - 1), :, columns(chunk)], sem.at[chunk])

        def rows_of(position):
            return pl.ds(pl.multiple_of(16 * position, 16), 16)

        for chunk in range(CHUNKS):
            part = columns(chunk)
            value = x2[x, :, part] + jnp.dot(
                heads, wo[1, :, :, :, part].reshape(512, cw), preferred_element_type=jnp.float32
            )
            entering = jnp.where(layer == 0, 0.0, sx[x, :, part].astype(jnp.float32))
            value = value - gy[y, :, part] * entering
            d_out[:, part] = value
            dsend[:, part] = value.astype(jnp.bfloat16)
            for k in ydeltas:
                start(
                    dsend.at[rows_of(ring_y[k]), columns(chunk)], drecv.at[y, :, columns(chunk)],
                    y1_ss.at[chunk], y1_rs.at[chunk], at_y(k),
                )
        drecv[y] = dsend[rows_of(y), :]
        for copy in product_coming:
            copy.wait_recv()
        for copy in sends:
            copy.wait_send()
        for chunk in range(CHUNKS):
            all_of(drecv, ny, chunk, y1_rs)
            total = jnp.zeros((16, cw), jnp.float32)
            for k in range(ny):
                total = gy[k, :, columns(chunk)] * total + drecv[k, :, columns(chunk)].astype(jnp.float32)
            trecv[z, :, columns(chunk)] = total.astype(jnp.bfloat16)
            for k in zdeltas:
                piece = trecv.at[z, :, columns(chunk)]
                start(piece, piece, z_ss.at[chunk], z_rs.at[chunk], at_z(k))
        for chunk in range(CHUNKS):
            all_of(drecv, ny, chunk, y1_ss)
        for chunk in range(CHUNKS):
            all_of(trecv, nz, chunk, z_rs)
            carry = jnp.zeros((16, cw), jnp.float32)
            for k in range(nz):
                longer = pz[k, :, columns(chunk)] * carry + trecv[k, :, columns(chunk)].astype(jnp.float32)
                carry = jnp.where(k < z, longer, carry)
            for k in range(ny):
                csend[k, :, columns(chunk)] = carry.astype(jnp.bfloat16)
                carry = gy[k, :, columns(chunk)] * carry + drecv[k, :, columns(chunk)].astype(jnp.float32)
            crecv[rows_of(y), columns(chunk)] = csend[y, :, columns(chunk)]
            for k in ydeltas:
                start(
                    csend.at[ring_y[k], :, columns(chunk)], crecv.at[rows_of(y), columns(chunk)],
                    y2_ss.at[chunk], y2_rs.at[chunk], at_y(k),
                )
        for chunk in range(CHUNKS):
            all_of(trecv, nz, chunk, z_ss)
        for j in range(NX):

            @pl.when(x != j)
            def _(copy=home[j]):
                copy.wait_send()

        for chunk in range(CHUNKS):
            all_of(csend, ny, chunk, y2_rs)
        c_out[...] = crecv[...]
        for chunk in range(CHUNKS):
            all_of(csend, ny, chunk, y2_ss)

    bf16, f32 = jnp.bfloat16, jnp.float32
    dma = pltpu.SemaphoreType.DMA
    scratch = [
        pltpu.VMEM((NX, 128, D), bf16),
        pltpu.VMEM((2, NX, 2, 128, 384), bf16),
        pltpu.VMEM((2, NX, 2, 64, D), bf16),
        pltpu.VMEM((2, NB, 128, 256), bf16),
        pltpu.VMEM((NX, 256, 128), bf16),
        pltpu.VMEM((NX, NX, 128, 128), bf16),
        pltpu.VMEM((NX, 128, 128), bf16),
        pltpu.VMEM((NX, 128, 128), bf16),
        pltpu.VMEM((NX, 128, D), f32),
        pltpu.VMEM((NX, 128, 640), f32),
        pltpu.VMEM((NB, 1, 128), jnp.int32),
        pltpu.VMEM((2, D), f32),
        pltpu.VMEM((ny, 1, D), f32),
        pltpu.VMEM((nz, 1, D), f32),
        pltpu.VMEM((128, D), bf16),
        pltpu.VMEM((ny, 16, D), bf16),
        pltpu.VMEM((nz, 16, D), bf16),
        pltpu.VMEM((ny, 16, D), bf16),
        pltpu.VMEM((128, D), bf16),
        dma((12,)),
        dma((2, 4, 3)), dma((2, 4, 3)), dma((2,)), dma((2,)),
        dma((4, 2)), dma((4, 2)), dma((8,)), dma((8,)),
        dma((2, 4, 2)), dma((2, 4, 2)), dma((2, 4)), dma((2, 4)),
        dma((2, 4)), dma((2, 4)), dma((4, 4)), dma((4, 4)), dma((4,)), dma((4,)),
        dma((8,)), dma((8,)), dma((8,)), dma((8,)),
        dma((CHUNKS,)), dma((CHUNKS,)), dma((CHUNKS,)), dma((CHUNKS,)), dma((CHUNKS,)), dma((CHUNKS,)),
    ]
    anywhere, vmem = pl.BlockSpec(memory_space=pltpu.HBM), pl.BlockSpec(memory_space=pltpu.VMEM)
    return pl.pallas_call(
        kernel,
        out_shape=(jax.ShapeDtypeStruct((128, D), bf16), jax.ShapeDtypeStruct((128, D), f32)),
        in_specs=[anywhere] * 6,
        out_specs=(vmem, vmem),
        scratch_shapes=scratch,
        compiler_params=pltpu.CompilerParams(
            collective_id=0, has_side_effects=True, vmem_limit_bytes=40 << 20
        ),
        cost_estimate=pl.CostEstimate(
            flops=3_000_000_000, bytes_accessed=4_000_000, transcendentals=2_000_000
        ),
    )


def solution(mesh):
    layers = mesh.shape["layer"]
    ny = min(RING, layers)
    nz = layers // ny
    call = make_kernel(ny, nz)

    def per_device(states, w_qkv, w_out, gains, coarse_gain, doc_ids):
        hold = [pltpu.with_memory_space_constraint(v, pltpu.HBM) for v in (states, w_qkv, w_out, gains, coarse_gain, doc_ids.reshape(1, -1))]
        entering, source = call(*hold)
        first = lax.axis_index("layer") == 0
        entering = entering.astype(jnp.float32)
        state = states[0].astype(jnp.float32)
        corrected = entering + jnp.where(first, state, 0.0)
        ends = coarse_gain * entering + source
        return corrected[None], ends[None]

    in_specs = (
        P("layer", "tok", None),
        P("layer", "tok", None),
        P("layer", "tok", None),
        P("layer", None),
        P("layer", None),
        P("tok"),
    )
    out_specs = (P("layer", "tok", None), P("layer", "tok", None))
    return jax.shard_map(
        per_device, mesh=mesh, in_specs=in_specs, out_specs=out_specs, check_vma=False
    )
```
